128 devices in a mesh: row: 8 (over z_hi, x), col: 16 (over y, z_lo, core).
Axes of the slice: x: 4, y: 4, z: 4 (z_hi: 2, z_lo: 2; z = z_hi * 2 + z_lo), core: 2. Of those that a mesh axis runs over, the one named last changes fastest.
Arguments:
- activations: bfloat16 [20480, 768], P(('row', 'col')), may hold values from -6 to 6
- signals: bfloat16 [20480, 768], P(('row', 'col')), may hold values from -6 to 6
- labels: int32 [20480], P(('row', 'col')), may hold values from 0 to 344
- coefficients: float32 [345, 20480], P(None, ('row', 'col')), may hold values from -6 to 6
Outputs:
- updated: float32 [345, 20480], P(None, ('row', 'col'))
The draws below stay inside these ranges and needn't reach their ends.
All inputs are finite; a program needn't handle non-finite values.
Results may differ from the reference program's by a relative error of at most 0.0003.
Values may be sent and summed in bfloat16 or wider, within the bound.
No kernel may reach another device: no remote copies, remote signals or barrier semaphores. Data moves between devices by JAX's collectives and lax.ppermute only.
A program may use at most 128 MiB of HBM per device.

```python
import jax
import jax.numpy as jnp
from jax import lax

FEAT = 768
CLASSES = 345
EXAMPLES = 20480
N_COL = 16


def place_ends(values, key, least, largest):
    shape = values.shape
    index_at = [jax.random.randint(jax.random.fold_in(key, axis), (), 0, shape[axis]) for axis in range(len(shape))]
    values = values.at[tuple(index_at)].set(least)
    longest = shape.index(max(shape))
    index_at[longest] = (index_at[longest] + 1) % shape[longest]
    return values.at[tuple(index_at)].set(largest)


def block_scale(rng, extent, split, least, top_value):
    loudness, own = 1.0, jax.random.fold_in(rng, 6)
    for axis_at, shards_of in split:
        heights = jnp.exp(jax.random.uniform(jax.random.fold_in(own, axis_at), (shards_of,), jnp.float32, least / len(split), top_value / len(split)))
        loudness = loudness * jnp.repeat(heights, extent[axis_at] // shards_of).reshape([-1 if axis == axis_at else 1 for axis in range(len(extent))])
    return loudness


def bell_draw(rng, shape, spread, most, pieces=(), held_as=jnp.bfloat16):
    values = spread * jax.random.normal(rng, shape, jnp.float32)
    if pieces:
        values = values * block_scale(rng, shape, pieces, -0.22, 0.18)
    return jnp.clip(values, -most, most).astype(held_as)


def setup_inputs(seed: int = 0) -> dict:
    key_of = jax.random.split(jax.random.key(seed), 5)
    return {
        "activations": bell_draw(key_of[0], (EXAMPLES, FEAT), 1.0, 6.0, ((0, 128),)),
        "signals": bell_draw(key_of[1], (EXAMPLES, FEAT), 1.0, 6.0, ((0, 128),)),
        "labels": place_ends(jax.random.randint(key_of[2], (EXAMPLES,), 0, CLASSES), jax.random.fold_in(key_of[2], 1), 0, CLASSES - 1).astype(jnp.int32),
        "coefficients": bell_draw(key_of[3], (CLASSES, EXAMPLES), 1.0, 6.0, ((1, 128),), jnp.float32),
    }


damping = 0.8
ridge = 0.1


def reference(activations, signals, labels, coefficients):
    block = EXAMPLES // N_COL
    act_blocks = activations.reshape(N_COL, block, FEAT)
    sig_blocks = signals.reshape(N_COL, block, FEAT)

    def one_block(pair):
        act_part, sig_part = pair
        gram_a = jnp.dot(activations, act_part.T, preferred_element_type=jnp.float32) / FEAT
        gram_s = jnp.dot(signals, sig_part.T, preferred_element_type=jnp.float32) / FEAT
        kernel = gram_a * gram_s
        return jnp.dot(coefficients, kernel, precision=lax.Precision.HIGHEST, preferred_element_type=jnp.float32)

    parts = lax.map(one_block, (act_blocks, sig_blocks))
    product = jnp.transpose(parts, (1, 0, 2)).reshape(CLASSES, EXAMPLES)
    classes = jnp.arange(CLASSES, dtype=jnp.int32)
    targets = (labels[None, :] == classes[:, None]).astype(jnp.float32) - 1.0 / CLASSES
    return coefficients + damping * (targets - product - ridge * coefficients)
```

```python
import functools

import jax
import jax.numpy as jnp
from jax import lax
from jax.experimental import pallas as pl
from jax.experimental.pallas import tpu as pltpu
from jax.sharding import PartitionSpec as P

FEAT = 768
CLASSES = 345
LANES = 384
OWN = 160
AXES = ("row", "col")

damping = 0.8
ridge = 0.1

f32, bf16 = jnp.float32, jnp.bfloat16
NT = (((1,), (1,)), ((), ()))
NN = (((1,), (0,)), ((), ()))


def encode(x, y, z, core):
    return ((((z >> 1) * 4 + x) * 4 + y) * 2 + (z & 1)) * 2 + core


def decode(index):
    return (index >> 4) & 3, (index >> 2) & 3, (index >> 6) * 2 + ((index >> 1) & 1), index & 1


def moves(dx=0, dy=0, far=0, near=0, other=0):
    pairs = []
    for index in range(128):
        x, y, z, core = decode(index)
        if far:
            z = 3 - z
        if near:
            z = z ^ 1
        pairs.append((index, encode((x + dx) % 4, (y + dy) % 4, z, core ^ other)))
    return pairs


def send(value, **move):
    return lax.ppermute(value, AXES, moves(**move))


def dot(a, b, dims):
    return lax.dot_general(a, b, dims, preferred_element_type=f32)


def gram_kernel(*refs):
    right_in, left_in, coef_in = refs[:8], refs[8:24], refs[24]
    outs = refs[25:33]
    right, left, coef, split, total, sems = refs[33:]
    col = lax.axis_index("col")
    copies = []
    for i in range(8):
        copies.append(pltpu.make_async_copy(right_in[i], right.at[pl.ds(i * OWN, OWN)], sems.at[i]))
    for i in range(16):
        copies.append(pltpu.make_async_copy(left_in[i], left.at[pl.ds(i * OWN, OWN)], sems.at[8 + i]))
    y, near, core = col // 4, (col // 2) % 2, col % 2
    for i, (dy, dn, dc) in enumerate(LEFT):
        at = (((y + dy) % 4) * 2 + (near + dn) % 2) * 2 + (core + dc) % 2
        copies.append(
            pltpu.make_async_copy(
                coef_in.at[pl.ds(pl.multiple_of(at * OWN, OWN), OWN)], coef.at[pl.ds(i * OWN, OWN)], sems.at[24 + i]
            )
        )
    for copy in copies:
        copy.start()
    for copy in copies:
        copy.wait()
    split[...] = jnp.zeros_like(split)
    values = coef[...]
    high = values.astype(bf16)
    split[:, :CLASSES] = high
    split[:, LANES : LANES + CLASSES] = (values - high.astype(f32)).astype(bf16)

    rows, cols = 640, 512

    @pl.loop(0, 1280 // rows)
    def _(step):
        n = pl.ds(pl.multiple_of(step * rows, rows), rows)
        part = None
        for j in range(2560 // cols):
            m = pl.ds(j * cols, cols)
            gram_a = dot(right[n, :FEAT], left[m, :FEAT], NT)
            gram_s = dot(right[n, FEAT:], left[m, FEAT:], NT)
            kernel = gram_a * gram_s
            high = kernel.astype(bf16)
            low = (kernel - high.astype(f32)).astype(bf16)
            both = dot(high, split[m, :], NN)
            new = both[:, :LANES] + both[:, LANES:] + dot(low, split[m, :LANES], NN)
            part = new if part is None else part + new
        total[n, :] = part

    for i in range(8):
        outs[i][...] = total[pl.ds(i * OWN, OWN), :CLASSES]


LEFT = tuple((dy, dn, dc) for dc in (0, 1) for dy, dn in ((0, 0), (0, 1), (1, 0), (3, 0), (1, 1), (3, 1), (2, 0), (2, 1)))


def partial_sums(right, left, coefs):
    spec = pl.BlockSpec(memory_space=pl.ANY)
    return pl.pallas_call(
        gram_kernel,
        out_shape=[jax.ShapeDtypeStruct((OWN, CLASSES), f32)] * 8,
        in_specs=[spec] * 25,
        out_specs=[pl.BlockSpec(memory_space=pltpu.VMEM)] * 8,
        scratch_shapes=[
            pltpu.VMEM((1280, 2 * FEAT), bf16),
            pltpu.VMEM((2560, 2 * FEAT), bf16),
            pltpu.VMEM((2560, CLASSES), f32),
            pltpu.VMEM((2560, 2 * LANES), bf16),
            pltpu.VMEM((1280, LANES), f32),
            pltpu.SemaphoreType.DMA((40,)),
        ],
        cost_estimate=pl.CostEstimate(flops=17_000_000_000, bytes_accessed=16_000_000, transcendentals=0),
        compiler_params=pltpu.CompilerParams(vmem_limit_bytes=48 << 20),
        name="gram_product",
    )(*right, *left, coefs)


def ring_gather(own, axis, pair):
    up, down = {axis: 1}, {axis: -1}
    mate = send(own, **{pair: 1})
    left, right = send(own, **up), send(own, **down)
    mate_left, mate_right = send(mate, **up), send(mate, **down)
    across = send(left, **up)
    mate_across = send(mate_right, **down)
    return [own, mate, right, left, mate_right, mate_left, across, mate_across]


def shards(activations, signals, labels, coefficients):
    coefs = coefficients.T
    all_coefs = lax.all_gather(coefs, "col", axis=0, tiled=True)
    own = jnp.concatenate([activations, signals], axis=1)
    right = ring_gather(own, "dx", "far")
    near = ring_gather(own, "dy", "near")
    left = near + [send(block, other=1) for block in near]
    sums = partial_sums(right, left, all_coefs)
    product = sums[0]
    for part, (dx, far) in zip(sums[1:], ((0, 1), (1, 0), (-1, 0), (1, 1), (-1, 1), (2, 0), (2, 1))):
        product = product + send(part, dx=dx, far=far)
    product = product * (1.0 / (FEAT * FEAT))
    classes = jnp.arange(CLASSES, dtype=jnp.int32)
    targets = (labels[:, None] == classes[None, :]).astype(f32) - 1.0 / CLASSES
    return (coefs + damping * (targets - product - ridge * coefs)).T


def solution(mesh):
    in_specs = (P(AXES, None), P(AXES, None), P(AXES), P(None, AXES))
    return jax.shard_map(shards, mesh=mesh, in_specs=in_specs, out_specs=P(None, AXES), check_vma=False)
```

```python
import functools

import jax
import jax.numpy as jnp
from jax import lax
from jax.experimental import pallas as pl
from jax.experimental.pallas import tpu as pltpu
from jax.sharding import PartitionSpec as P

FEAT = 768
CLASSES = 345
LANES = 384
OWN = 160
AXES = ("row", "col")

damping = 0.8
ridge = 0.1

f32, bf16 = jnp.float32, jnp.bfloat16
NT = (((1,), (1,)), ((), ()))
NN = (((1,), (0,)), ((), ()))
VMEM = pl.BlockSpec(memory_space=pltpu.VMEM)


def encode(x, y, z, core):
    return ((((z >> 1) * 4 + x) * 4 + y) * 2 + (z & 1)) * 2 + core


def decode(index):
    return (index >> 4) & 3, (index >> 2) & 3, (index >> 6) * 2 + ((index >> 1) & 1), index & 1


def moves(group, dims):
    pairs = []
    for index in range(128):
        x, y, z, core = decode(index)
        place = {"x": x, "y": y, "z": z}
        for dim in dims:
            if dim == "c":
                core ^= 1
            else:
                place[dim] = 3 - place[dim] if group == "far" else place[dim] ^ 1
        pairs.append((index, encode(place["x"], place["y"], place["z"], core)))
    return pairs


def send(value, group, dims):
    return lax.ppermute(value, AXES, moves(group, dims))


def after(value, *others):
    return lax.optimization_barrier((value, *others))[0]


def dot(a, b, dims):
    return lax.dot_general(a, b, dims, preferred_element_type=f32)


def split_kernel(coef, split):
    split[...] = jnp.zeros_like(split)
    values = coef[...]
    high = values.astype(bf16)
    split[:, :CLASSES] = high
    split[:, LANES : LANES + CLASSES] = (values - high.astype(f32)).astype(bf16)


def split_coefs(coefs):
    return pl.pallas_call(
        split_kernel,
        out_shape=pltpu.VMEM((OWN, 2 * LANES), bf16),
        in_specs=[VMEM],
        out_specs=VMEM,
        compiler_params=pltpu.CompilerParams(vmem_limit_bytes=4 << 20),
        name="split_coefs",
    )(coefs)


def arrange_kernel(plan, n_in, *refs):
    for out, pieces in zip(refs[n_in:], plan):
        for source, row, out_row, out_col in pieces:
            out[out_row * OWN : (out_row + 1) * OWN, out_col * FEAT : (out_col + 1) * FEAT] = refs[source][
                row * OWN : (row + 1) * OWN, :
            ]


def arrange(outputs, name):
    arrays, plan, shapes = [], [], []

    def place(array):
        for i, known in enumerate(arrays):
            if known is array:
                return i
        arrays.append(array)
        return len(arrays) - 1

    for columns in outputs:
        plan.append(
            [
                (place(array), block, out_row, out_col)
                for out_col, column in enumerate(columns)
                for out_row, (array, block) in enumerate(column)
            ]
        )
        shapes.append(pltpu.VMEM((len(columns[0]) * OWN, len(columns) * FEAT), bf16))
    return pl.pallas_call(
        functools.partial(arrange_kernel, plan, len(arrays)),
        out_shape=shapes,
        in_specs=[VMEM] * len(arrays),
        out_specs=[VMEM] * len(shapes),
        compiler_params=pltpu.CompilerParams(vmem_limit_bytes=8 << 20),
        name=name,
    )(*arrays)


def block_kernel(plan, n_in, with_total, apart, rows, *refs):
    inputs, refs = refs[:n_in], refs[n_in:]
    total_in, refs = (refs[0], refs[1:]) if with_total else (None, refs)
    outs, (right, left, split) = refs[:-3], refs[-3:]
    targets = (right, left, split)
    for target, out_row, out_col, source, row, col in plan:
        targets[target][out_row * OWN : (out_row + 1) * OWN, out_col * FEAT : (out_col + 1) * FEAT] = inputs[source][
            row * OWN : (row + 1) * OWN, col * FEAT : (col + 1) * FEAT
        ]
    n_right, n_left = right.shape[0], left.shape[0]
    for start in range(0, n_right, rows):
        n = slice(start, start + rows)
        part = total_in[n, :] if with_total else None
        at = 0
        while at < n_left:
            size = min(512, n_left - at)
            m = slice(at, at + size)
            at += size
            gram_a = dot(right[n, :FEAT], left[m, :FEAT], NT)
            gram_s = dot(right[n, FEAT:], left[m, FEAT:], NT)
            kernel = gram_a * gram_s
            high = kernel.astype(bf16)
            low = (kernel - high.astype(f32)).astype(bf16)
            both = dot(high, split[m, :], NN)
            new = both[:, :LANES] + both[:, LANES:] + dot(low, split[m, :LANES], NN)
            part = new if part is None else part + new
        if apart:
            for i in range(rows // OWN):
                outs[start // OWN + i][...] = part[i * OWN : (i + 1) * OWN, :CLASSES]
        else:
            outs[0][n, :] = part


def partial_sums(right, left, total, apart, rows, name):
    arrays, plan = [], []

    def place(array):
        for i, known in enumerate(arrays):
            if known is array:
                return i
        arrays.append(array)
        return len(arrays) - 1

    for i, (act, sig) in enumerate(right):
        plan.append((0, i, 0, place(act[0]), act[1], act[2]))
        plan.append((0, i, 1, place(sig[0]), sig[1], sig[2]))
    for i, (act, sig, coef) in enumerate(left):
        plan.append((1, i, 0, place(act[0]), act[1], act[2]))
        plan.append((1, i, 1, place(sig[0]), sig[1], sig[2]))
        plan.append((2, i, 0, place(coef[0]), coef[1], coef[2]))
    n_right, n_left = len(right), len(left)
    if apart:
        out_shape = [pltpu.VMEM((OWN, CLASSES), f32)] * n_right
    else:
        out_shape = [pltpu.VMEM((n_right * OWN, LANES), f32)]
    pairs = n_right * n_left * OWN * OWN
    return pl.pallas_call(
        functools.partial(block_kernel, plan, len(arrays), total is not None, apart, rows),
        out_shape=out_shape,
        in_specs=[VMEM] * (len(arrays) + (total is not None)),
        out_specs=[VMEM] * len(out_shape),
        scratch_shapes=[
            pltpu.VMEM((n_right * OWN, 2 * FEAT), bf16),
            pltpu.VMEM((n_left * OWN, 2 * FEAT), bf16),
            pltpu.VMEM((n_left * OWN, 2 * LANES), bf16),
        ],
        cost_estimate=pl.CostEstimate(flops=pairs * 5400, bytes_accessed=8_000_000, transcendentals=0),
        compiler_params=pltpu.CompilerParams(vmem_limit_bytes=24 << 20),
        name=name,
    )(*arrays, *([] if total is None else [total]))


def shards(activations, signals, labels, coefficients):
    coefs = coefficients.T
    groups = ("far", "near")
    a, s, c = {}, {}, {}
    for g in groups:
        a[g, "x"] = send(activations, g, "x")
        s[g, "y"] = send(signals, g, "y")
    c0 = split_coefs(coefs)
    cz = send(c0, "near", "z")
    pairs = arrange(
        [[[(activations, 0), (a[g, "x"], 0)]] for g in groups]
        + [[[(signals, 0), (s[g, "y"], 0)]] for g in groups]
        + [[[(c0, 0), (cz, 0)]]]
        + [[[(activations, 0), (a["near", "x"], 0)], [(signals, 0), (s["near", "y"], 0)], [(c0, 0), (cz, 0)]]],
        "pairs",
    )
    a0x, s0y, c0z, own2 = dict(zip(groups, pairs[:2])), dict(zip(groups, pairs[2:4])), pairs[4], pairs[5]
    ay, sz = {}, {}
    for g in groups:
        ay[g] = send(a0x[g], g, "y")
        sz[g] = send(s0y[g], g, "z")
    cx = send(c0z, "near", "x")
    own2_mate = send(own2, "near", "c")
    ay["far"], ay["near"], sz["far"], sz["near"], cx = lax.optimization_barrier(
        (ay["far"], ay["near"], sz["far"], sz["near"], cx)
    )
    fours = arrange(
        [[[(a0x[g], 0), (ay[g], 0)]] for g in groups]
        + [[[(a0x[g], 1), (ay[g], 1)]] for g in groups]
        + [[[(ay["near"], 0), (ay["near"], 1)], [(sz["near"], 0), (sz["near"], 1)], [(cx, 0), (cx, 1)]]],
        "fours",
    )
    a0y, axxy, next2 = dict(zip(groups, fours[:2])), dict(zip(groups, fours[2:4])), fours[4]
    az, sx = {}, {}
    for g in groups:
        az[g] = send(after(a0y[g], own2_mate), g, "z")
        sx[g] = send(after(s0y[g], next2, own2_mate), g, "x")
    cy = send(after(c0z, next2, own2_mate), "near", "y")
    az["far"], az["near"], sx["far"], sx["near"], cy, next2 = lax.optimization_barrier(
        (az["far"], az["near"], sx["far"], sx["near"], cy, next2)
    )
    mates = [send(v, "near", "c") for v in (next2, az["near"], sx["near"], cy)]
    next2_mate, az_mate, sx_mate, cy_mate = mates
    axz, sxz = {}, {}
    for g in groups:
        axz[g] = send(after(axxy[g], cy), g, "z")
        sxz[g] = send(after(sz[g], cy), g, "x")
    cxy = send(after(cx, *mates), "near", "y")

    def blocks_of(g):
        act = {"": (a0x[g], 0, 0), "x": (a0x[g], 1, 0), "y": (ay[g], 0, 0), "xy": (ay[g], 1, 0)}
        act |= {"z": (az[g], 0, 0), "yz": (az[g], 1, 0), "xz": (axz[g], 0, 0), "xyz": (axz[g], 1, 0)}
        sig = {"": (s0y[g], 0, 0), "y": (s0y[g], 1, 0), "z": (sz[g], 0, 0), "yz": (sz[g], 1, 0)}
        sig |= {"x": (sx[g], 0, 0), "xy": (sx[g], 1, 0), "xz": (sxz[g], 0, 0), "xyz": (sxz[g], 1, 0)}
        return act, sig

    act, sig = blocks_of("far")
    right = {k: (act[k], sig[k]) for k in act}
    act, sig = blocks_of("near")
    coef = {"": (c0z, 0, 0), "z": (c0z, 1, 0), "x": (cx, 0, 0), "xz": (cx, 1, 0)}
    coef |= {"y": (cy, 0, 0), "yz": (cy, 1, 0), "xy": (cxy, 0, 0), "xyz": (cxy, 1, 0)}
    left = {k: (act[k], sig[k], coef[k]) for k in act}
    right_1 = [right[k] for k in ("", "x", "y", "xy", "z", "yz")]
    right_2 = [right[k] for k in ("xz", "xyz")]
    act_mate = {"": (own2_mate, 0, 0), "x": (own2_mate, 1, 0), "y": (next2_mate, 0, 0), "xy": (next2_mate, 1, 0)}
    act_mate |= {"z": (az_mate, 0, 0), "yz": (az_mate, 1, 0)}
    sig_mate = {"": (own2_mate, 0, 1), "y": (own2_mate, 1, 1), "z": (next2_mate, 0, 1), "yz": (next2_mate, 1, 1)}
    sig_mate |= {"x": (sx_mate, 0, 0), "xy": (sx_mate, 1, 0)}
    coef_mate = {"": (own2_mate, 0, 2), "z": (own2_mate, 1, 2), "x": (next2_mate, 0, 2), "xz": (next2_mate, 1, 2)}
    coef_mate |= {"y": (cy_mate, 0, 0), "yz": (cy_mate, 1, 0)}
    first = ("", "x", "y", "z", "yz")
    left_1 = [left[k] for k in first] + [(act_mate[k], sig_mate[k], coef_mate[k]) for k in first]
    (total_1,) = partial_sums(right_1, left_1, None, False, 480, "early")

    axz_mate, sxz_mate, cxy_mate = [send(after(v, total_1), "near", "c") for v in (axz["near"], sxz["near"], cxy)]
    act_mate |= {"xz": (axz_mate, 0, 0), "xyz": (axz_mate, 1, 0)}
    sig_mate |= {"xz": (sxz_mate, 0, 0), "xyz": (sxz_mate, 1, 0)}
    coef_mate |= {"xy": (cxy_mate, 0, 0), "xyz": (cxy_mate, 1, 0)}
    second = ("xy", "xz", "xyz")
    left_2 = [left[k] for k in second] + [(act_mate[k], sig_mate[k], coef_mate[k]) for k in second]
    (total_2,) = partial_sums(right_2, left_1, None, False, 320, "late_right")
    sum_xz, sum_xyz = partial_sums(right_2, left_2, total_2, True, 320, "late_both")
    total_1 = after(total_1, sum_xz)
    own, sum_x, sum_y, sum_xy, sum_z, sum_yz = partial_sums(right_1, left_2, total_1, True, 480, "late_left")

    product = own
    for part, dims in ((sum_xyz, "xyz"), (sum_xz, "xz"), (sum_xy, "xy"), (sum_yz, "yz"), (sum_x, "x"), (sum_y, "y"), (sum_z, "z")):
        product = product + send(part, "far", dims)
    product = product * (1.0 / (FEAT * FEAT))
    classes = jnp.arange(CLASSES, dtype=jnp.int32)
    targets = (labels[:, None] == classes[None, :]).astype(f32) - 1.0 / CLASSES
    return (coefs + damping * (targets - product - ridge * coefs)).T


def solution(mesh):
    in_specs = (P(AXES, None), P(AXES, None), P(AXES), P(None, AXES))
    return jax.shard_map(shards, mesh=mesh, in_specs=in_specs, out_specs=P(None, AXES), check_vma=False)
```

```python
import functools

import jax
import jax.numpy as jnp
from jax import lax
from jax.experimental import pallas as pl
from jax.experimental.pallas import tpu as pltpu
from jax.sharding import PartitionSpec as P

FEAT = 768
CLASSES = 345
LANES = 384
OWN = 160
AXES = ("row", "col")

damping = 0.8
ridge = 0.1

f32, bf16 = jnp.float32, jnp.bfloat16
NT = (((1,), (1,)), ((), ()))
NN = (((1,), (0,)), ((), ()))
VMEM = pl.BlockSpec(memory_space=pltpu.VMEM)


def encode(x, y, z, core):
    return ((((z >> 1) * 4 + x) * 4 + y) * 2 + (z & 1)) * 2 + core


def decode(index):
    return (index >> 4) & 3, (index >> 2) & 3, (index >> 6) * 2 + ((index >> 1) & 1), index & 1


def moves(group, dims):
    pairs = []
    for index in range(128):
        x, y, z, core = decode(index)
        place = {"x": x, "y": y, "z": z}
        for dim in dims:
            if dim == "c":
                core ^= 1
            else:
                place[dim] = 3 - place[dim] if group == "far" else place[dim] ^ 1
        pairs.append((index, encode(place["x"], place["y"], place["z"], core)))
    return pairs


def send(value, group, dims):
    return lax.ppermute(value, AXES, moves(group, dims))


def after(value, *others):
    return lax.optimization_barrier((value, *others))[0]


def dot(a, b, dims):
    return lax.dot_general(a, b, dims, preferred_element_type=f32)


def stage_kernel(act, sig, coef, act_out, sig_out, split):
    act_out[...] = act[...]
    sig_out[...] = sig[...]
    split[...] = jnp.zeros_like(split)
    values = coef[...]
    high = values.astype(bf16)
    split[:, :CLASSES] = high
    split[:, LANES : LANES + CLASSES] = (values - high.astype(f32)).astype(bf16)


def stage(act, sig, coefs):
    return pl.pallas_call(
        stage_kernel,
        out_shape=[pltpu.VMEM((OWN, FEAT), bf16), pltpu.VMEM((OWN, FEAT), bf16), pltpu.VMEM((OWN, 2 * LANES), bf16)],
        in_specs=[VMEM] * 3,
        out_specs=[VMEM] * 3,
        compiler_params=pltpu.CompilerParams(vmem_limit_bytes=4 << 20),
        name="stage",
    )(act, sig, coefs)


def arrange_kernel(plan, n_in, *refs):
    for out, pieces in zip(refs[n_in:], plan):
        for source, row, out_row, out_col in pieces:
            out[out_row * OWN : (out_row + 1) * OWN, out_col * FEAT : (out_col + 1) * FEAT] = refs[source][
                row * OWN : (row + 1) * OWN, :
            ]


def arrange(outputs, name):
    arrays, plan, shapes = [], [], []

    def place(array):
        for i, known in enumerate(arrays):
            if known is array:
                return i
        arrays.append(array)
        return len(arrays) - 1

    for columns in outputs:
        plan.append(
            [
                (place(array), block, out_row, out_col)
                for out_col, column in enumerate(columns)
                for out_row, (array, block) in enumerate(column)
            ]
        )
        shapes.append(pltpu.VMEM((len(columns[0]) * OWN, len(columns) * FEAT), bf16))
    return pl.pallas_call(
        functools.partial(arrange_kernel, plan, len(arrays)),
        out_shape=shapes,
        in_specs=[VMEM] * len(arrays),
        out_specs=[VMEM] * len(shapes),
        compiler_params=pltpu.CompilerParams(vmem_limit_bytes=8 << 20),
        name=name,
    )(*arrays)


def block_kernel(plan, n_in, total_row, apart, keep_left, ready_left, n_right, rows, *refs):
    inputs, refs = refs[:n_in], refs[n_in:]
    if ready_left:
        (left, split), refs = refs[:2], refs[2:]
    total_in, refs = (refs[0], refs[1:]) if total_row is not None else (None, refs)
    outs, refs = (refs[:n_right], refs[n_right:]) if apart else (refs[:1], refs[1:])
    if not ready_left:
        (left, split), refs = refs[:2], refs[2:]
    (right,) = refs
    targets = (right, left, split)
    for target, out_row, out_col, source, row, col in plan:
        targets[target][out_row * OWN : (out_row + 1) * OWN, out_col * FEAT : (out_col + 1) * FEAT] = inputs[source][
            row * OWN : (row + 1) * OWN, col * FEAT : (col + 1) * FEAT
        ]
    n_left = left.shape[0]
    for start in range(0, n_right * OWN, rows):
        n = slice(start, start + rows)
        part = None if total_in is None else total_in[total_row + start : total_row + start + rows, :]
        at = 0
        while at < n_left:
            size = min(512, n_left - at)
            m = slice(at, at + size)
            at += size
            gram_a = dot(right[n, :FEAT], left[m, :FEAT], NT)
            gram_s = dot(right[n, FEAT:], left[m, FEAT:], NT)
            kernel = gram_a * gram_s
            high = kernel.astype(bf16)
            low = (kernel - high.astype(f32)).astype(bf16)
            both = dot(high, split[m, :], NN)
            new = both[:, :LANES] + both[:, LANES:] + dot(low, split[m, :LANES], NN)
            part = new if part is None else part + new
        if apart:
            for i in range(rows // OWN):
                outs[start // OWN + i][...] = part[i * OWN : (i + 1) * OWN, :CLASSES]
        else:
            outs[0][n, :] = part


def partial_sums(right, left, total, apart, rows, name, keep_left=False, ready=None):
    arrays, plan = [], []

    def place(array):
        for i, known in enumerate(arrays):
            if known is array:
                return i
        arrays.append(array)
        return len(arrays) - 1

    for i, (act, sig) in enumerate(right):
        plan.append((0, i, 0, place(act[0]), act[1], act[2]))
        plan.append((0, i, 1, place(sig[0]), sig[1], sig[2]))
    for i, (act, sig, coef) in enumerate(left):
        plan.append((1, i, 0, place(act[0]), act[1], act[2]))
        plan.append((1, i, 1, place(sig[0]), sig[1], sig[2]))
        plan.append((2, i, 0, place(coef[0]), coef[1], coef[2]))
    n_in, n_right = len(arrays), len(right)
    left_rows = ready[0].shape[0] if ready else len(left) * OWN
    if apart:
        out_shape = [pltpu.VMEM((OWN, CLASSES), f32)] * n_right
    else:
        out_shape = [pltpu.VMEM((n_right * OWN, LANES), f32)]
    left_shape = [pltpu.VMEM((left_rows, 2 * FEAT), bf16), pltpu.VMEM((left_rows, 2 * LANES), bf16)]
    scratch = [pltpu.VMEM((n_right * OWN, 2 * FEAT), bf16)]
    if ready:
        arrays += ready
    elif keep_left:
        out_shape = out_shape + left_shape
    else:
        scratch = left_shape + scratch
    if total is not None:
        arrays.append(total[0])
    pairs = n_right * OWN * left_rows
    return pl.pallas_call(
        functools.partial(
            block_kernel, plan, n_in, None if total is None else total[1], apart, keep_left, bool(ready), n_right, rows
        ),
        out_shape=out_shape,
        in_specs=[VMEM] * len(arrays),
        out_specs=[VMEM] * len(out_shape),
        scratch_shapes=scratch,
        cost_estimate=pl.CostEstimate(flops=pairs * 5400, bytes_accessed=8_000_000, transcendentals=0),
        compiler_params=pltpu.CompilerParams(vmem_limit_bytes=24 << 20),
        name=name,
    )(*arrays)


def shards(activations, signals, labels, coefficients):
    coefs = coefficients.T
    groups = ("far", "near")
    a, s, c = {}, {}, {}
    for g in groups:
        a[g, "x"] = send(activations, g, "x")
        s[g, "y"] = send(signals, g, "y")
    act_own, sig_own, c0 = stage(activations, signals, coefs)
    cz = send(c0, "near", "z")
    pairs = arrange(
        [[[(act_own, 0), (a[g, "x"], 0)]] for g in groups]
        + [[[(sig_own, 0), (s[g, "y"], 0)]] for g in groups]
        + [[[(c0, 0), (cz, 0)]]]
        + [[[(act_own, 0), (a["near", "x"], 0)], [(sig_own, 0), (s["near", "y"], 0)], [(c0, 0), (cz, 0)]]],
        "pairs",
    )
    a0x, s0y, c0z, own2 = dict(zip(groups, pairs[:2])), dict(zip(groups, pairs[2:4])), pairs[4], pairs[5]
    ay, sz = {}, {}
    for g in groups:
        ay[g] = send(a0x[g], g, "y")
        sz[g] = send(s0y[g], g, "z")
    cx = send(c0z, "near", "x")
    ay["far"], ay["near"], sz["far"], sz["near"], cx, own2 = lax.optimization_barrier(
        (ay["far"], ay["near"], sz["far"], sz["near"], cx, own2)
    )
    own2_mate = send(own2, "near", "c")
    fours = arrange(
        [[[(a0x[g], 0), (ay[g], 0)]] for g in groups]
        + [[[(a0x[g], 1), (ay[g], 1)]] for g in groups]
        + [[[(ay["near"], 0), (ay["near"], 1)], [(sz["near"], 0), (sz["near"], 1)], [(cx, 0), (cx, 1)]]],
        "fours",
    )
    a0y, axxy, next2 = dict(zip(groups, fours[:2])), dict(zip(groups, fours[2:4])), fours[4]
    az, sx = {}, {}
    for g in groups:
        az[g] = send(a0y[g], g, "z")
        sx[g] = send(after(s0y[g], next2), g, "x")
    cy = send(after(c0z, next2, own2_mate), "near", "y")
    az["far"], az["near"], sx["far"], sx["near"], cy, next2 = lax.optimization_barrier(
        (az["far"], az["near"], sx["far"], sx["near"], cy, next2)
    )
    mates = [send(v, "near", "c") for v in (next2, az["near"], sx["near"], cy)]
    next2_mate, az_mate, sx_mate, cy_mate = mates
    axz, sxz = {}, {}
    for g in groups:
        axz[g] = send(after(axxy[g], cy), g, "z")
        sxz[g] = send(after(sz[g], cy), g, "x")
    cxy = send(after(cx, *mates), "near", "y")

    def blocks_of(g):
        act = {"": (a0x[g], 0, 0), "x": (a0x[g], 1, 0), "y": (ay[g], 0, 0), "xy": (ay[g], 1, 0)}
        act |= {"z": (az[g], 0, 0), "yz": (az[g], 1, 0), "xz": (axz[g], 0, 0), "xyz": (axz[g], 1, 0)}
        sig = {"": (s0y[g], 0, 0), "y": (s0y[g], 1, 0), "z": (sz[g], 0, 0), "yz": (sz[g], 1, 0)}
        sig |= {"x": (sx[g], 0, 0), "xy": (sx[g], 1, 0), "xz": (sxz[g], 0, 0), "xyz": (sxz[g], 1, 0)}
        return act, sig

    act, sig = blocks_of("far")
    right = {k: (act[k], sig[k]) for k in act}
    act, sig = blocks_of("near")
    coef = {"": (c0z, 0, 0), "z": (c0z, 1, 0), "x": (cx, 0, 0), "xz": (cx, 1, 0)}
    coef |= {"y": (cy, 0, 0), "yz": (cy, 1, 0), "xy": (cxy, 0, 0), "xyz": (cxy, 1, 0)}
    left = {k: (act[k], sig[k], coef[k]) for k in act}
    right_1 = [right[k] for k in ("xy", "yz", "x", "y", "z", "")]
    right_2 = [right[k] for k in ("xyz", "xz")]
    act_mate = {"": (own2_mate, 0, 0), "x": (own2_mate, 1, 0), "y": (next2_mate, 0, 0), "xy": (next2_mate, 1, 0)}
    act_mate |= {"z": (az_mate, 0, 0), "yz": (az_mate, 1, 0)}
    sig_mate = {"": (own2_mate, 0, 1), "y": (own2_mate, 1, 1), "z": (next2_mate, 0, 1), "yz": (next2_mate, 1, 1)}
    sig_mate |= {"x": (sx_mate, 0, 0), "xy": (sx_mate, 1, 0)}
    coef_mate = {"": (own2_mate, 0, 2), "z": (own2_mate, 1, 2), "x": (next2_mate, 0, 2), "xz": (next2_mate, 1, 2)}
    coef_mate |= {"y": (cy_mate, 0, 0), "yz": (cy_mate, 1, 0)}
    first = ("", "x", "y", "z", "yz")
    left_1 = [left[k] for k in first] + [(act_mate[k], sig_mate[k], coef_mate[k]) for k in first]
    (total_1,) = partial_sums(right_1, left_1, None, False, 480, "early")

    axz_mate, sxz_mate, cxy_mate = [send(after(v, total_1), "near", "c") for v in (axz["near"], sxz["near"], cxy)]
    act_mate |= {"xz": (axz_mate, 0, 0), "xyz": (axz_mate, 1, 0)}
    sig_mate |= {"xz": (sxz_mate, 0, 0), "xyz": (sxz_mate, 1, 0)}
    coef_mate |= {"xy": (cxy_mate, 0, 0), "xyz": (cxy_mate, 1, 0)}
    second = ("xy", "xz", "xyz")
    left_2 = [left[k] for k in second] + [(act_mate[k], sig_mate[k], coef_mate[k]) for k in second]
    (total_2,) = partial_sums(right_2, left_1, None, False, 320, "late_right")
    got = {}
    sum_xyz, sum_xz, *ready = partial_sums(right_2, left_2, (total_2, 0), True, 320, "late_1", keep_left=True)
    got["xyz"], got["xz"] = send(sum_xyz, "far", "xyz"), send(sum_xz, "far", "xz")
    total_1 = after(total_1, sum_xz)
    sum_xy, sum_yz = partial_sums(right_1[:2], (), (total_1, 0), True, 320, "late_2", ready=ready)
    got["xy"], got["yz"] = send(sum_xy, "far", "xy"), send(sum_yz, "far", "yz")
    total_1 = after(total_1, sum_yz)
    sum_x, sum_y = partial_sums(right_1[2:4], (), (total_1, 2 * OWN), True, 320, "late_3", ready=ready)
    got["x"] = send(sum_x, "far", "x")
    total_1 = after(total_1, sum_y)
    sum_z, own = partial_sums(right_1[4:], (), (total_1, 4 * OWN), True, 320, "late_4", ready=ready)
    got["y"] = send(after(sum_y, got["xz"]), "far", "y")
    got["z"] = send(after(sum_z, got["xyz"]), "far", "z")

    product = own
    for part in got.values():
        product = product + part
    product = product * (1.0 / (FEAT * FEAT))
    classes = jnp.arange(CLASSES, dtype=jnp.int32)
    targets = (labels[:, None] == classes[None, :]).astype(f32) - 1.0 / CLASSES
    return (coefs + damping * (targets - product - ridge * coefs)).T


def solution(mesh):
    in_specs = (P(AXES, None), P(AXES, None), P(AXES), P(None, AXES))
    return jax.shard_map(shards, mesh=mesh, in_specs=in_specs, out_specs=P(None, AXES), check_vma=False)
```

```python
import functools

import jax
import jax.numpy as jnp
from jax import lax
from jax.experimental import pallas as pl
from jax.experimental.pallas import tpu as pltpu
from jax.sharding import PartitionSpec as P

FEAT = 768
CLASSES = 345
LANES = 384
OWN = 160
AXES = ("row", "col")

damping = 0.8
ridge = 0.1

f32, bf16 = jnp.float32, jnp.bfloat16
NT = (((1,), (1,)), ((), ()))
NN = (((1,), (0,)), ((), ()))
VMEM = pl.BlockSpec(memory_space=pltpu.VMEM)


def encode(x, y, z, core):
    return ((((z >> 1) * 4 + x) * 4 + y) * 2 + (z & 1)) * 2 + core


def decode(index):
    return (index >> 4) & 3, (index >> 2) & 3, (index >> 6) * 2 + ((index >> 1) & 1), index & 1


def moves(group, dims):
    pairs = []
    for index in range(128):
        x, y, z, core = decode(index)
        place = {"x": x, "y": y, "z": z}
        for dim in dims:
            if dim == "c":
                core ^= 1
            else:
                place[dim] = 3 - place[dim] if group == "far" else place[dim] ^ 1
        pairs.append((index, encode(place["x"], place["y"], place["z"], core)))
    return pairs


def send(value, group, dims):
    return lax.ppermute(value, AXES, moves(group, dims))


def after(value, *others):
    return lax.optimization_barrier((value, *others))[0]


def dot(a, b, dims):
    return lax.dot_general(a, b, dims, preferred_element_type=f32)


def split_kernel(coef, split):
    split[...] = jnp.zeros_like(split)
    values = coef[...]
    high = values.astype(bf16)
    split[:, :CLASSES] = high
    split[:, LANES : LANES + CLASSES] = (values - high.astype(f32)).astype(bf16)


def split_coefs(coefs):
    return pl.pallas_call(
        split_kernel,
        out_shape=pltpu.VMEM((OWN, 2 * LANES), bf16),
        in_specs=[VMEM],
        out_specs=VMEM,
        compiler_params=pltpu.CompilerParams(vmem_limit_bytes=4 << 20),
        name="split_coefs",
    )(coefs)


def arrange_kernel(plan, n_in, *refs):
    for out, pieces in zip(refs[n_in:], plan):
        for source, row, out_row, out_col in pieces:
            out[out_row * OWN : (out_row + 1) * OWN, out_col * FEAT : (out_col + 1) * FEAT] = refs[source][
                row * OWN : (row + 1) * OWN, :
            ]


def arrange(outputs, name):
    arrays, plan, shapes = [], [], []

    def place(array):
        for i, known in enumerate(arrays):
            if known is array:
                return i
        arrays.append(array)
        return len(arrays) - 1

    for columns in outputs:
        plan.append(
            [
                (place(array), block, out_row, out_col)
                for out_col, column in enumerate(columns)
                for out_row, (array, block) in enumerate(column)
            ]
        )
        shapes.append(pltpu.VMEM((len(columns[0]) * OWN, len(columns) * FEAT), bf16))
    return pl.pallas_call(
        functools.partial(arrange_kernel, plan, len(arrays)),
        out_shape=shapes,
        in_specs=[VMEM] * len(arrays),
        out_specs=[VMEM] * len(shapes),
        compiler_params=pltpu.CompilerParams(vmem_limit_bytes=8 << 20),
        name=name,
    )(*arrays)


def block_kernel(plan, n_in, total_row, apart, keep_left, ready_left, n_right, rows, *refs):
    inputs, refs = refs[:n_in], refs[n_in:]
    if ready_left:
        (left, split), refs = refs[:2], refs[2:]
    total_in, refs = (refs[0], refs[1:]) if total_row is not None else (None, refs)
    outs, refs = (refs[:n_right], refs[n_right:]) if apart else (refs[:1], refs[1:])
    if not ready_left:
        (left, split), refs = refs[:2], refs[2:]
    (right,) = refs
    targets = (right, left, split)
    for target, out_row, out_col, source, row, col in plan:
        targets[target][out_row * OWN : (out_row + 1) * OWN, out_col * FEAT : (out_col + 1) * FEAT] = inputs[source][
            row * OWN : (row + 1) * OWN, col * FEAT : (col + 1) * FEAT
        ]
    n_left = left.shape[0]
    for start in range(0, n_right * OWN, rows):
        n = slice(start, start + rows)
        part = None if total_in is None else total_in[total_row + start : total_row + start + rows, :]
        at = 0
        while at < n_left:
            size = min(512, n_left - at)
            m = slice(at, at + size)
            at += size
            gram_a = dot(right[n, :FEAT], left[m, :FEAT], NT)
            gram_s = dot(right[n, FEAT:], left[m, FEAT:], NT)
            kernel = gram_a * gram_s
            high = kernel.astype(bf16)
            low = (kernel - high.astype(f32)).astype(bf16)
            both = dot(high, split[m, :], NN)
            new = both[:, :LANES] + both[:, LANES:] + dot(low, split[m, :LANES], NN)
            part = new if part is None else part + new
        if apart:
            for i in range(rows // OWN):
                outs[start // OWN + i][...] = part[i * OWN : (i + 1) * OWN, :CLASSES]
        else:
            outs[0][n, :] = part


def partial_sums(right, left, total, apart, rows, name, keep_left=False, ready=None):
    arrays, plan = [], []

    def place(array):
        for i, known in enumerate(arrays):
            if known is array:
                return i
        arrays.append(array)
        return len(arrays) - 1

    for i, (act, sig) in enumerate(right):
        plan.append((0, i, 0, place(act[0]), act[1], act[2]))
        plan.append((0, i, 1, place(sig[0]), sig[1], sig[2]))
    for i, (act, sig, coef) in enumerate(left):
        plan.append((1, i, 0, place(act[0]), act[1], act[2]))
        plan.append((1, i, 1, place(sig[0]), sig[1], sig[2]))
        plan.append((2, i, 0, place(coef[0]), coef[1], coef[2]))
    n_in, n_right = len(arrays), len(right)
    left_rows = ready[0].shape[0] if ready else len(left) * OWN
    if apart:
        out_shape = [pltpu.VMEM((OWN, CLASSES), f32)] * n_right
    else:
        out_shape = [pltpu.VMEM((n_right * OWN, LANES), f32)]
    left_shape = [pltpu.VMEM((left_rows, 2 * FEAT), bf16), pltpu.VMEM((left_rows, 2 * LANES), bf16)]
    scratch = [pltpu.VMEM((n_right * OWN, 2 * FEAT), bf16)]
    if ready:
        arrays += ready
    elif keep_left:
        out_shape = out_shape + left_shape
    else:
        scratch = left_shape + scratch
    if total is not None:
        arrays.append(total[0])
    pairs = n_right * OWN * left_rows
    return pl.pallas_call(
        functools.partial(
            block_kernel, plan, n_in, None if total is None else total[1], apart, keep_left, bool(ready), n_right, rows
        ),
        out_shape=out_shape,
        in_specs=[VMEM] * len(arrays),
        out_specs=[VMEM] * len(out_shape),
        scratch_shapes=scratch,
        cost_estimate=pl.CostEstimate(flops=pairs * 5400, bytes_accessed=8_000_000, transcendentals=0),
        compiler_params=pltpu.CompilerParams(vmem_limit_bytes=24 << 20),
        name=name,
    )(*arrays)


def shards(activations, signals, labels, coefficients):
    coefs = coefficients.T
    groups = ("far", "near")
    a, s, c = {}, {}, {}
    for g in groups:
        a[g, "x"] = send(activations, g, "x")
        s[g, "y"] = send(signals, g, "y")
    c0 = split_coefs(coefs)
    cz = send(c0, "near", "z")
    act_own, sig_own = arrange([[[(after(v, c0), 0)]] for v in (activations, signals)], "own_rows")

    def together(*values):
        return lax.optimization_barrier(values)

    a["far", "x"], a["near", "x"], s["far", "y"], s["near", "y"], cz = together(
        a["far", "x"], a["near", "x"], s["far", "y"], s["near", "y"], cz
    )

    pairs = arrange(
        [[[(act_own, 0), (a[g, "x"], 0)]] for g in groups]
        + [[[(sig_own, 0), (s[g, "y"], 0)]] for g in groups]
        + [[[(c0, 0), (cz, 0)]]]
        + [[[(act_own, 0), (a["near", "x"], 0)], [(sig_own, 0), (s["near", "y"], 0)], [(c0, 0), (cz, 0)]]],
        "pairs",
    )
    a0x, s0y, c0z, own2 = dict(zip(groups, pairs[:2])), dict(zip(groups, pairs[2:4])), pairs[4], pairs[5]
    own2_mate = send(own2, "near", "c")
    ay, sz = {}, {}
    for g in groups:
        ay[g] = send(a0x[g], g, "y")
        sz[g] = send(s0y[g], g, "z")
    cx = send(after(c0z, own2_mate), "near", "x")
    ay["far"], ay["near"], sz["far"], sz["near"], cx = together(ay["far"], ay["near"], sz["far"], sz["near"], cx)
    n = "near"
    turned = arrange(
        [[[(a0x[g], k), (ay[g], k)]] for k in (0, 1) for g in groups]
        + [[[(ay[n], 0), (ay[n], 1)], [(sz[n], 0), (sz[n], 1)], [(cx, 0), (cx, 1)]]],
        "turn",
    )
    a0y, axxy, next2 = dict(zip(groups, turned[:2])), dict(zip(groups, turned[2:4])), turned[4]
    next2_mate = send(next2, n, "c")
    az, sx = {}, {}
    for g in groups:
        sx[g] = send(after(s0y[g], sz[g]), g, "x")
        az[g] = send(a0y[g], g, "z")
    cy = send(after(c0z, cx, next2_mate), n, "y")
    az["far"], az[n], sx["far"], sx[n], cy, axxy["far"], axxy[n], sz["far"], sz[n], cx = together(
        az["far"], az[n], sx["far"], sx[n], cy, axxy["far"], axxy[n], sz["far"], sz[n], cx
    )
    az_mate, sx_mate, cy_mate = small = [send(v, n, "c") for v in (az[n], sx[n], cy)]
    axz, sxz = {}, {}
    axz[n] = send(axxy[n], n, "z")
    sxz[n] = send(sz[n], n, "x")
    cxy = send(after(cx, *small), n, "y")
    axz["far"] = send(after(axxy["far"], *small), "far", "z")
    sxz["far"] = send(after(sz["far"], *small), "far", "x")

    def blocks_of(g):
        act = {"": (a0x[g], 0, 0), "x": (a0x[g], 1, 0), "y": (ay[g], 0, 0), "xy": (ay[g], 1, 0)}
        act |= {"z": (az[g], 0, 0), "yz": (az[g], 1, 0), "xz": (axz[g], 0, 0), "xyz": (axz[g], 1, 0)}
        sig = {"": (s0y[g], 0, 0), "y": (s0y[g], 1, 0), "z": (sz[g], 0, 0), "yz": (sz[g], 1, 0)}
        sig |= {"x": (sx[g], 0, 0), "xy": (sx[g], 1, 0), "xz": (sxz[g], 0, 0), "xyz": (sxz[g], 1, 0)}
        return act, sig

    act, sig = blocks_of("far")
    right = {k: (act[k], sig[k]) for k in act}
    act, sig = blocks_of("near")
    coef = {"": (c0z, 0, 0), "z": (c0z, 1, 0), "x": (cx, 0, 0), "xz": (cx, 1, 0)}
    coef |= {"y": (cy, 0, 0), "yz": (cy, 1, 0), "xy": (cxy, 0, 0), "xyz": (cxy, 1, 0)}
    left = {k: (act[k], sig[k], coef[k]) for k in act}
    right_1 = [right[k] for k in ("xy", "yz", "x", "y", "z", "")]
    right_2 = [right[k] for k in ("xyz", "xz")]
    act_mate = {"": (own2_mate, 0, 0), "x": (own2_mate, 1, 0), "y": (next2_mate, 0, 0), "xy": (next2_mate, 1, 0)}
    act_mate |= {"z": (az_mate, 0, 0), "yz": (az_mate, 1, 0)}
    sig_mate = {"": (own2_mate, 0, 1), "y": (own2_mate, 1, 1), "z": (next2_mate, 0, 1), "yz": (next2_mate, 1, 1)}
    sig_mate |= {"x": (sx_mate, 0, 0), "xy": (sx_mate, 1, 0)}
    coef_mate = {"": (own2_mate, 0, 2), "z": (own2_mate, 1, 2), "x": (next2_mate, 0, 2), "xz": (next2_mate, 1, 2)}
    coef_mate |= {"y": (cy_mate, 0, 0), "yz": (cy_mate, 1, 0)}
    first = ("", "x", "y", "z", "yz")
    left_1 = [left[k] for k in first] + [(act_mate[k], sig_mate[k], coef_mate[k]) for k in first]
    (total_1,) = partial_sums(right_1, left_1, None, False, 480, "early")

    axz_mate, sxz_mate, cxy_mate = [send(after(v, total_1), "near", "c") for v in (axz["near"], sxz["near"], cxy)]
    act_mate |= {"xz": (axz_mate, 0, 0), "xyz": (axz_mate, 1, 0)}
    sig_mate |= {"xz": (sxz_mate, 0, 0), "xyz": (sxz_mate, 1, 0)}
    coef_mate |= {"xy": (cxy_mate, 0, 0), "xyz": (cxy_mate, 1, 0)}
    second = ("xy", "xz", "xyz")
    left_2 = [left[k] for k in second] + [(act_mate[k], sig_mate[k], coef_mate[k]) for k in second]
    (total_2,) = partial_sums(right_2, left_1, None, False, 320, "late_right")
    sum_xyz, sum_xz, *ready = partial_sums(right_2, left_2, (total_2, 0), True, 320, "late_1", keep_left=True)
    got_xyz, part_x = send(sum_xyz, "far", "xyz"), send(sum_xz, "far", "z")
    total_1 = after(total_1, sum_xz)
    sum_xy, sum_yz = partial_sums(right_1[:2], (), (total_1, 0), True, 320, "late_2", ready=ready)
    part_y, part_z = send(sum_xy, "far", "x"), send(sum_yz, "far", "y")
    total_1 = after(total_1, sum_yz)
    sum_x, sum_y = partial_sums(right_1[2:4], (), (total_1, 2 * OWN), True, 320, "late_3", ready=ready)
    total_1 = after(total_1, sum_y, got_xyz)
    sum_z, own = partial_sums(right_1[4:], (), (total_1, 4 * OWN), True, 320, "late_4", ready=ready)
    got_x = send(after(sum_x + part_x, own), "far", "x")
    got_y = send(after(sum_y + part_y, own), "far", "y")
    got_z = send(after(sum_z + part_z, own), "far", "z")

    product = own + got_xyz + got_x + got_y + got_z
    product = product * (1.0 / (FEAT * FEAT))
    classes = jnp.arange(CLASSES, dtype=jnp.int32)
    targets = (labels[:, None] == classes[None, :]).astype(f32) - 1.0 / CLASSES
    return (coefs + damping * (targets - product - ridge * coefs)).T


def solution(mesh):
    in_specs = (P(AXES, None), P(AXES, None), P(AXES), P(None, AXES))
    return jax.shard_map(shards, mesh=mesh, in_specs=in_specs, out_specs=P(None, AXES), check_vma=False)
```

```python
import functools

import jax
import jax.numpy as jnp
from jax import lax
from jax.experimental import pallas as pl
from jax.experimental.pallas import tpu as pltpu
from jax.sharding import PartitionSpec as P

FEAT = 768
CLASSES = 345
LANES = 384
OWN = 160
AXES = ("row", "col")

damping = 0.8
ridge = 0.1

f32, bf16 = jnp.float32, jnp.bfloat16
NT = (((1,), (1,)), ((), ()))
NN = (((1,), (0,)), ((), ()))
VMEM = pl.BlockSpec(memory_space=pltpu.VMEM)


def encode(x, y, z, core):
    return ((((z >> 1) * 4 + x) * 4 + y) * 2 + (z & 1)) * 2 + core


def decode(index):
    return (index >> 4) & 3, (index >> 2) & 3, (index >> 6) * 2 + ((index >> 1) & 1), index & 1


def moves(group, dims):
    pairs = []
    for index in range(128):
        x, y, z, core = decode(index)
        place = {"x": x, "y": y, "z": z}
        for dim in dims:
            if dim == "c":
                core ^= 1
            else:
                place[dim] = 3 - place[dim] if group == "far" else place[dim] ^ 1
        pairs.append((index, encode(place["x"], place["y"], place["z"], core)))
    return pairs


def send(value, group, dims):
    return lax.ppermute(value, AXES, moves(group, dims))


def after(value, *others):
    return lax.optimization_barrier((value, *others))[0]


def dot(a, b, dims):
    return lax.dot_general(a, b, dims, preferred_element_type=f32)


def split_kernel(coef, split):
    split[...] = jnp.zeros_like(split)
    values = coef[...]
    high = values.astype(bf16)
    split[:, :CLASSES] = high
    split[:, LANES : LANES + CLASSES] = (values - high.astype(f32)).astype(bf16)


def split_coefs(coefs):
    return pl.pallas_call(
        split_kernel,
        out_shape=pltpu.VMEM((OWN, 2 * LANES), bf16),
        in_specs=[VMEM],
        out_specs=VMEM,
        compiler_params=pltpu.CompilerParams(vmem_limit_bytes=4 << 20),
        name="split_coefs",
    )(coefs)


def arrange_kernel(plan, n_in, *refs):
    for out, pieces in zip(refs[n_in:], plan):
        for source, row, out_row, out_col in pieces:
            out[out_row * OWN : (out_row + 1) * OWN, out_col * FEAT : (out_col + 1) * FEAT] = refs[source][
                row * OWN : (row + 1) * OWN, :
            ]


def arrange(outputs, name):
    arrays, plan, shapes = [], [], []

    def place(array):
        for i, known in enumerate(arrays):
            if known is array:
                return i
        arrays.append(array)
        return len(arrays) - 1

    for columns in outputs:
        plan.append(
            [
                (place(array), block, out_row, out_col)
                for out_col, column in enumerate(columns)
                for out_row, (array, block) in enumerate(column)
            ]
        )
        shapes.append(pltpu.VMEM((len(columns[0]) * OWN, len(columns) * FEAT), bf16))
    return pl.pallas_call(
        functools.partial(arrange_kernel, plan, len(arrays)),
        out_shape=shapes,
        in_specs=[VMEM] * len(arrays),
        out_specs=[VMEM] * len(shapes),
        compiler_params=pltpu.CompilerParams(vmem_limit_bytes=8 << 20),
        name=name,
    )(*arrays)


def block_kernel(plan, n_in, parts, left_ready, apart, *refs):
    inputs, refs = refs[:n_in], refs[n_in:]
    if left_ready:
        (left, split), refs = refs[:2], refs[2:]
    rights, totals = [None] * len(parts), [None] * len(parts)
    for i, (ready, _, _, total_row) in enumerate(parts):
        if ready:
            rights[i], refs = refs[0], refs[1:]
        if total_row is not None:
            totals[i], refs = refs[0], refs[1:]
    n_outs = sum(part[2] for part in parts) // OWN if apart else len(parts)
    outs, refs = refs[:n_outs], refs[n_outs:]
    if not left_ready:
        (left, split), refs = refs[:2], refs[2:]
    for i, (ready, _, _, _) in enumerate(parts):
        if not ready:
            rights[i], refs = refs[0], refs[1:]
    targets = (left, split, *rights)
    for target, out_row, out_col, source, row, col in plan:
        targets[target][out_row * OWN : (out_row + 1) * OWN, out_col * FEAT : (out_col + 1) * FEAT] = inputs[source][
            row * OWN : (row + 1) * OWN, col * FEAT : (col + 1) * FEAT
        ]
    done = 0
    for i, (_, first, count, total_row) in enumerate(parts):
        right = rights[i]
        rows = 480 if count % 480 == 0 else 320
        for start in range(0, count, rows):
            n = slice(first + start, first + start + rows)
            part = None
            if total_row is not None:
                part = totals[i][total_row + start : total_row + start + rows, :]
            for at in range(0, left.shape[0], 512):
                m = slice(at, min(at + 512, left.shape[0]))
                gram_a = dot(right[n, :FEAT], left[m, :FEAT], NT)
                gram_s = dot(right[n, FEAT:], left[m, FEAT:], NT)
                kernel = gram_a * gram_s
                high = kernel.astype(bf16)
                low = (kernel - high.astype(f32)).astype(bf16)
                both = dot(high, split[m, :], NN)
                new = both[:, :LANES] + both[:, LANES:] + dot(low, split[m, :LANES], NN)
                part = new if part is None else part + new
            if apart:
                for k in range(rows // OWN):
                    outs[done + k][...] = part[k * OWN : (k + 1) * OWN, :CLASSES]
                done += rows // OWN
            else:
                outs[i][start : start + rows, :] = part


def partial_sums(rights, left, apart, name):
    arrays, plan = [], []

    def place(array):
        for i, known in enumerate(arrays):
            if known is array:
                return i
        arrays.append(array)
        return len(arrays) - 1

    left_ready = isinstance(left, tuple)
    if not left_ready:
        for i, (act, sig, coef) in enumerate(left):
            plan.append((0, i, 0, place(act[0]), act[1], act[2]))
            plan.append((0, i, 1, place(sig[0]), sig[1], sig[2]))
            plan.append((1, i, 0, place(coef[0]), coef[1], coef[2]))
    for target, (blocks, *_) in enumerate(rights):
        if isinstance(blocks, list):
            for i, (act, sig) in enumerate(blocks):
                plan.append((2 + target, i, 0, place(act[0]), act[1], act[2]))
                plan.append((2 + target, i, 1, place(sig[0]), sig[1], sig[2]))
    n_in = len(arrays)
    left_rows = left[0].shape[0] if left_ready else len(left) * OWN
    if left_ready:
        arrays += left
    parts, laid = [], []
    for blocks, first, count, total, total_row in rights:
        ready = not isinstance(blocks, list)
        parts.append((ready, first, count, None if total is None else total_row))
        if ready:
            arrays.append(blocks)
        else:
            laid.append(pltpu.VMEM((len(blocks) * OWN, 2 * FEAT), bf16))
        if total is not None:
            arrays.append(total)
    if not left_ready:
        laid = [pltpu.VMEM((left_rows, 2 * FEAT), bf16), pltpu.VMEM((left_rows, 2 * LANES), bf16)] + laid
    if apart:
        sums = [pltpu.VMEM((OWN, CLASSES), f32)] * (sum(part[2] for part in parts) // OWN)
    else:
        sums = [pltpu.VMEM((part[2], LANES), f32) for part in parts]
    outs = pl.pallas_call(
        functools.partial(block_kernel, plan, n_in, parts, left_ready, apart),
        out_shape=sums + laid,
        in_specs=[VMEM] * len(arrays),
        out_specs=[VMEM] * (len(sums) + len(laid)),
        cost_estimate=pl.CostEstimate(
            flops=sum(part[2] for part in parts) * left_rows * 5400, bytes_accessed=1_000_000, transcendentals=0
        ),
        compiler_params=pltpu.CompilerParams(vmem_limit_bytes=16 << 20),
        name=name,
    )(*arrays)
    return outs[: len(sums)], outs[len(sums) :]


def shards(activations, signals, labels, coefficients):
    coefs = coefficients.T
    groups = ("far", "near")
    a, s, c = {}, {}, {}
    for g in groups:
        a[g, "x"] = send(activations, g, "x")
        s[g, "y"] = send(signals, g, "y")
    c0 = split_coefs(coefs)
    cz = send(c0, "near", "z")
    act_own, sig_own = arrange([[[(after(v, c0), 0)]] for v in (activations, signals)], "own_rows")

    def together(*values):
        return lax.optimization_barrier(values)

    a["far", "x"], a["near", "x"], s["far", "y"], s["near", "y"], cz = together(
        a["far", "x"], a["near", "x"], s["far", "y"], s["near", "y"], cz
    )

    pairs = arrange(
        [[[(act_own, 0), (a[g, "x"], 0)]] for g in groups]
        + [[[(sig_own, 0), (s[g, "y"], 0)]] for g in groups]
        + [[[(c0, 0), (cz, 0)]]],
        "pairs",
    )
    a0x, s0y, c0z = dict(zip(groups, pairs[:2])), dict(zip(groups, pairs[2:4])), pairs[4]
    ay, sz = {}, {}
    for g in groups:
        ay[g] = send(a0x[g], g, "y")
        sz[g] = send(s0y[g], g, "z")
    cx = send(c0z, "near", "x")
    ay["far"], ay["near"], sz["far"], sz["near"], cx = together(ay["far"], ay["near"], sz["far"], sz["near"], cx)
    turned = arrange(
        [[[(a0x[g], k), (ay[g], k)]] for k in (0, 1) for g in groups],
        "turn",
    )
    a0y, axxy = dict(zip(groups, turned[:2])), dict(zip(groups, turned[2:]))
    az, sx = {}, {}
    for g in groups:
        sx[g] = send(after(s0y[g], sz[g]), g, "x")
    cy = send(after(c0z, cx), "near", "y")
    for g in groups:
        az[g] = send(a0y[g], g, "z")
    n = "near"
    (four,) = arrange(
        [
            [
                [(a0x[n], 0), (a0x[n], 1), (ay[n], 0), (ay[n], 1)],
                [(s0y[n], 0), (s0y[n], 1), (sz[n], 0), (sz[n], 1)],
                [(c0z, 0), (c0z, 1), (cx, 0), (cx, 1)],
            ]
        ],
        "four",
    )
    az["far"], az[n], sx["far"], sx[n], cy, four, axxy[n], sz[n], axxy["far"], sz["far"] = together(
        az["far"], az[n], sx["far"], sx[n], cy, four, axxy[n], sz[n], axxy["far"], sz["far"]
    )
    az_mate, sx_mate, cy_mate = small = [send(v, n, "c") for v in (az[n], sx[n], cy)]
    axz, sxz = {}, {}
    axz[n] = send(axxy[n], n, "z")
    sxz[n] = send(sz[n], n, "x")
    axz["far"] = send(after(axxy["far"], *small), "far", "z")
    sxz["far"] = send(after(sz["far"], *small), "far", "x")
    four_mate = send(after(four, *small), n, "c")
    cxy = send(after(cx, cy, four_mate), n, "y")

    def blocks_of(g):
        act = {"": (a0x[g], 0, 0), "x": (a0x[g], 1, 0), "y": (ay[g], 0, 0), "xy": (ay[g], 1, 0)}
        act |= {"z": (az[g], 0, 0), "yz": (az[g], 1, 0), "xz": (axz[g], 0, 0), "xyz": (axz[g], 1, 0)}
        sig = {"": (s0y[g], 0, 0), "y": (s0y[g], 1, 0), "z": (sz[g], 0, 0), "yz": (sz[g], 1, 0)}
        sig |= {"x": (sx[g], 0, 0), "xy": (sx[g], 1, 0), "xz": (sxz[g], 0, 0), "xyz": (sxz[g], 1, 0)}
        return act, sig

    act, sig = blocks_of("far")
    right = {k: (act[k], sig[k]) for k in act}
    act, sig = blocks_of("near")
    coef = {"": (c0z, 0, 0), "z": (c0z, 1, 0), "x": (cx, 0, 0), "xz": (cx, 1, 0)}
    coef |= {"y": (cy, 0, 0), "yz": (cy, 1, 0), "xy": (cxy, 0, 0), "xyz": (cxy, 1, 0)}
    left = {k: (act[k], sig[k], coef[k]) for k in act}
    right_1 = [right[k] for k in ("xy", "yz", "x", "y", "z", "")]
    right_2 = [right[k] for k in ("xz", "xyz")]
    first, second = ("", "x", "y", "z", "yz"), ("xy", "xz", "xyz")

    coef[""] = (after(c0z, *small), 0, 0)
    act_mate = {"": (four_mate, 0, 0), "x": (four_mate, 1, 0), "y": (four_mate, 2, 0), "xy": (four_mate, 3, 0)}
    act_mate |= {"z": (az_mate, 0, 0), "yz": (az_mate, 1, 0)}
    sig_mate = {"": (four_mate, 0, 1), "y": (four_mate, 1, 1), "z": (four_mate, 2, 1), "yz": (four_mate, 3, 1)}
    sig_mate |= {"x": (sx_mate, 0, 0), "xy": (sx_mate, 1, 0)}
    coef_mate = {"": (four_mate, 0, 2), "z": (four_mate, 1, 2), "x": (four_mate, 2, 2), "xz": (four_mate, 3, 2)}
    coef_mate |= {"y": (cy_mate, 0, 0), "yz": (cy_mate, 1, 0)}
    left_1 = [(left[k][0], left[k][1], coef[k]) for k in first]
    left_1 += [(act_mate[k], sig_mate[k], coef_mate[k]) for k in first]
    (total_1,), (rows_1, coefs_1, wide_1) = partial_sums([(right_1, 0, 960, None, 0)], left_1, False, "early")
    axz_mate, sxz_mate = [send(after(v, total_1), n, "c") for v in (axz[n], sxz[n])]
    cxy_mate = send(cxy, n, "c")
    (total_2,), (wide_2,) = partial_sums(
        [(right_2, 0, 320, None, 0)], (after(rows_1, total_1), coefs_1), False, "early_right"
    )
    left["xy"] = (left["xy"][0], left["xy"][1], (after(cxy, total_2), 0, 0))
    (total_1, total_2), _ = partial_sums(
        [(wide_1, 0, 960, total_1, 0), (wide_2, 0, 320, total_2, 0)], [left[k] for k in second], False, "second_own"
    )
    act_mate |= {"xz": (axz_mate, 0, 0), "xyz": (axz_mate, 1, 0)}
    sig_mate |= {"xz": (sxz_mate, 0, 0), "xyz": (sxz_mate, 1, 0)}
    coef_mate |= {"xy": (cxy_mate, 0, 0), "xyz": (cxy_mate, 1, 0)}
    left_mate = {k: (act_mate[k], sig_mate[k], coef_mate[k]) for k in second}

    (sum_xz, sum_xyz, sum_xy, sum_yz), (rows_2, coefs_2) = partial_sums(
        [(wide_2, 0, 320, total_2, 0), (wide_1, 0, 320, total_1, 0)], [left_mate[k] for k in second], True, "second_mate_far"
    )
    part_x, part_y, part_z = send(sum_xz, "far", "z"), send(sum_xy, "far", "x"), send(sum_yz, "far", "y")
    got_xyz = send(sum_xyz, "far", "xyz")
    (sum_x, sum_y, sum_z, own), _ = partial_sums(
        [(wide_1, 320, 640, total_1, 320)], (after(rows_2, sum_xz), coefs_2), True, "second_mate_near"
    )
    got_x = send(after(sum_x + part_x, own), "far", "x")
    got_y = send(after(sum_y + part_y, own), "far", "y")
    got_z = send(after(sum_z + part_z, own), "far", "z")

    product = own + got_xyz + got_x + got_y + got_z
    product = product * (1.0 / (FEAT * FEAT))
    classes = jnp.arange(CLASSES, dtype=jnp.int32)
    targets = (labels[:, None] == classes[None, :]).astype(f32) - 1.0 / CLASSES
    return (coefs + damping * (targets - product - ridge * coefs)).T


def solution(mesh):
    in_specs = (P(AXES, None), P(AXES, None), P(AXES), P(None, AXES))
    return jax.shard_map(shards, mesh=mesh, in_specs=in_specs, out_specs=P(None, AXES), check_vma=False)
```

```python
import functools

import jax
import jax.numpy as jnp
from jax import lax
from jax.experimental import pallas as pl
from jax.experimental.pallas import tpu as pltpu
from jax.sharding import PartitionSpec as P

FEAT = 768
CLASSES = 345
LANES = 384
OWN = 160
AXES = ("row", "col")

damping = 0.8
ridge = 0.1

f32, bf16 = jnp.float32, jnp.bfloat16
NT = (((1,), (1,)), ((), ()))
NN = (((1,), (0,)), ((), ()))
VMEM = pl.BlockSpec(memory_space=pltpu.VMEM)


def encode(x, y, z, core):
    return ((((z >> 1) * 4 + x) * 4 + y) * 2 + (z & 1)) * 2 + core


def decode(index):
    return (index >> 4) & 3, (index >> 2) & 3, (index >> 6) * 2 + ((index >> 1) & 1), index & 1


def moves(group, dims):
    pairs = []
    for index in range(128):
        x, y, z, core = decode(index)
        place = {"x": x, "y": y, "z": z}
        for dim in dims:
            if dim == "c":
                core ^= 1
            else:
                place[dim] = 3 - place[dim] if group == "far" else place[dim] ^ 1
        pairs.append((index, encode(place["x"], place["y"], place["z"], core)))
    return pairs


def send(value, group, dims):
    return lax.ppermute(value, AXES, moves(group, dims))


def after(value, *others):
    return lax.optimization_barrier((value, *others))[0]


def dot(a, b, dims):
    return lax.dot_general(a, b, dims, preferred_element_type=f32)


def split_kernel(coef, split):
    split[...] = jnp.zeros_like(split)
    values = coef[...]
    high = values.astype(bf16)
    split[:, :CLASSES] = high
    split[:, LANES : LANES + CLASSES] = (values - high.astype(f32)).astype(bf16)


def split_coefs(coefs):
    return pl.pallas_call(
        split_kernel,
        out_shape=pltpu.VMEM((OWN, 2 * LANES), bf16),
        in_specs=[VMEM],
        out_specs=VMEM,
        compiler_params=pltpu.CompilerParams(vmem_limit_bytes=4 << 20),
        name="split_coefs",
    )(coefs)


def arrange_kernel(plan, n_in, *refs):
    for out, pieces in zip(refs[n_in:], plan):
        for source, row, out_row, out_col in pieces:
            out[out_row * OWN : (out_row + 1) * OWN, out_col * FEAT : (out_col + 1) * FEAT] = refs[source][
                row * OWN : (row + 1) * OWN, :
            ]


def arrange(outputs, name):
    arrays, plan, shapes = [], [], []

    def place(array):
        for i, known in enumerate(arrays):
            if known is array:
                return i
        arrays.append(array)
        return len(arrays) - 1

    for columns in outputs:
        plan.append(
            [
                (place(array), block, out_row, out_col)
                for out_col, column in enumerate(columns)
                for out_row, (array, block) in enumerate(column)
            ]
        )
        shapes.append(pltpu.VMEM((len(columns[0]) * OWN, len(columns) * FEAT), bf16))
    return pl.pallas_call(
        functools.partial(arrange_kernel, plan, len(arrays)),
        out_shape=shapes,
        in_specs=[VMEM] * len(arrays),
        out_specs=[VMEM] * len(shapes),
        compiler_params=pltpu.CompilerParams(vmem_limit_bytes=8 << 20),
        name=name,
    )(*arrays)


def block_kernel(plan, n_in, parts, left_ready, apart, *refs):
    inputs, refs = refs[:n_in], refs[n_in:]
    if left_ready:
        (left, split), refs = refs[:2], refs[2:]
    rights, totals = [None] * len(parts), [None] * len(parts)
    for i, (ready, _, _, total_row) in enumerate(parts):
        if ready:
            rights[i], refs = refs[0], refs[1:]
        if total_row is not None:
            totals[i], refs = refs[0], refs[1:]
    n_outs = sum(part[2] for part in parts) // OWN if apart else len(parts)
    outs, refs = refs[:n_outs], refs[n_outs:]
    if not left_ready:
        (left, split), refs = refs[:2], refs[2:]
    for i, (ready, _, _, _) in enumerate(parts):
        if not ready:
            rights[i], refs = refs[0], refs[1:]
    targets = (left, split, *rights)
    for target, out_row, out_col, source, row, col in plan:
        targets[target][out_row * OWN : (out_row + 1) * OWN, out_col * FEAT : (out_col + 1) * FEAT] = inputs[source][
            row * OWN : (row + 1) * OWN, col * FEAT : (col + 1) * FEAT
        ]
    done = 0
    for i, (_, first, count, total_row) in enumerate(parts):
        right = rights[i]
        rows = 480 if count % 480 == 0 else 320
        for start in range(0, count, rows):
            n = slice(first + start, first + start + rows)
            part = None
            if total_row is not None:
                part = totals[i][total_row + start : total_row + start + rows, :]
            for at in range(0, left.shape[0], 512):
                m = slice(at, min(at + 512, left.shape[0]))
                gram_a = dot(right[n, :FEAT], left[m, :FEAT], NT)
                gram_s = dot(right[n, FEAT:], left[m, FEAT:], NT)
                kernel = gram_a * gram_s
                high = kernel.astype(bf16)
                low = (kernel - high.astype(f32)).astype(bf16)
                both = dot(high, split[m, :], NN)
                new = both[:, :LANES] + both[:, LANES:] + dot(low, split[m, :LANES], NN)
                part = new if part is None else part + new
            if apart:
                for k in range(rows // OWN):
                    outs[done + k][...] = part[k * OWN : (k + 1) * OWN, :CLASSES]
                done += rows // OWN
            else:
                outs[i][start : start + rows, :] = part


def partial_sums(rights, left, apart, name):
    arrays, plan = [], []

    def place(array):
        for i, known in enumerate(arrays):
            if known is array:
                return i
        arrays.append(array)
        return len(arrays) - 1

    left_ready = isinstance(left, tuple)
    if not left_ready:
        for i, (act, sig, coef) in enumerate(left):
            plan.append((0, i, 0, place(act[0]), act[1], act[2]))
            plan.append((0, i, 1, place(sig[0]), sig[1], sig[2]))
            plan.append((1, i, 0, place(coef[0]), coef[1], coef[2]))
    for target, (blocks, *_) in enumerate(rights):
        if isinstance(blocks, list):
            for i, (act, sig) in enumerate(blocks):
                plan.append((2 + target, i, 0, place(act[0]), act[1], act[2]))
                plan.append((2 + target, i, 1, place(sig[0]), sig[1], sig[2]))
    n_in = len(arrays)
    left_rows = left[0].shape[0] if left_ready else len(left) * OWN
    if left_ready:
        arrays += left
    parts, laid = [], []
    for blocks, first, count, total, total_row in rights:
        ready = not isinstance(blocks, list)
        parts.append((ready, first, count, None if total is None else total_row))
        if ready:
            arrays.append(blocks)
        else:
            laid.append(pltpu.VMEM((len(blocks) * OWN, 2 * FEAT), bf16))
        if total is not None:
            arrays.append(total)
    if not left_ready:
        laid = [pltpu.VMEM((left_rows, 2 * FEAT), bf16), pltpu.VMEM((left_rows, 2 * LANES), bf16)] + laid
    if apart:
        sums = [pltpu.VMEM((OWN, CLASSES), f32)] * (sum(part[2] for part in parts) // OWN)
    else:
        sums = [pltpu.VMEM((part[2], LANES), f32) for part in parts]
    outs = pl.pallas_call(
        functools.partial(block_kernel, plan, n_in, parts, left_ready, apart),
        out_shape=sums + laid,
        in_specs=[VMEM] * len(arrays),
        out_specs=[VMEM] * (len(sums) + len(laid)),
        cost_estimate=pl.CostEstimate(
            flops=sum(part[2] for part in parts) * left_rows * 5400, bytes_accessed=1_000_000, transcendentals=0
        ),
        compiler_params=pltpu.CompilerParams(vmem_limit_bytes=16 << 20),
        name=name,
    )(*arrays)
    return outs[: len(sums)], outs[len(sums) :]


def shards(activations, signals, labels, coefficients):
    coefs = coefficients.T
    groups = ("far", "near")
    a, s, c = {}, {}, {}
    for g in groups:
        a[g, "x"] = send(activations, g, "x")
        s[g, "y"] = send(signals, g, "y")
    c0 = split_coefs(coefs)
    cz = send(c0, "near", "z")
    act_own, sig_own = arrange([[[(after(v, c0), 0)]] for v in (activations, signals)], "own_rows")

    def together(*values):
        return lax.optimization_barrier(values)

    a["far", "x"], a["near", "x"], s["far", "y"], s["near", "y"], cz = together(
        a["far", "x"], a["near", "x"], s["far", "y"], s["near", "y"], cz
    )

    pairs = arrange(
        [[[(act_own, 0), (a[g, "x"], 0)]] for g in groups]
        + [[[(sig_own, 0), (s[g, "y"], 0)]] for g in groups]
        + [[[(c0, 0), (cz, 0)]]],
        "pairs",
    )
    a0x, s0y, c0z = dict(zip(groups, pairs[:2])), dict(zip(groups, pairs[2:4])), pairs[4]
    ay, sz = {}, {}
    for g in groups:
        ay[g] = send(a0x[g], g, "y")
        sz[g] = send(s0y[g], g, "z")
    cx = send(c0z, "near", "x")
    ay["far"], ay["near"], sz["far"], sz["near"], cx = together(ay["far"], ay["near"], sz["far"], sz["near"], cx)
    turned = arrange(
        [[[(a0x[g], k), (ay[g], k)]] for k in (0, 1) for g in groups],
        "turn",
    )
    a0y, axxy = dict(zip(groups, turned[:2])), dict(zip(groups, turned[2:]))
    az, sx = {}, {}
    for g in groups:
        sx[g] = send(after(s0y[g], sz[g]), g, "x")
    cy = send(after(c0z, cx), "near", "y")
    for g in groups:
        az[g] = send(a0y[g], g, "z")
    n = "near"
    (four,) = arrange(
        [
            [
                [(a0x[n], 0), (a0x[n], 1), (ay[n], 0), (ay[n], 1)],
                [(s0y[n], 0), (s0y[n], 1), (sz[n], 0), (sz[n], 1)],
                [(c0z, 0), (c0z, 1), (cx, 0), (cx, 1)],
            ]
        ],
        "four",
    )
    az["far"], az[n], sx["far"], sx[n], cy, four, axxy[n], sz[n], axxy["far"], sz["far"] = together(
        az["far"], az[n], sx["far"], sx[n], cy, four, axxy[n], sz[n], axxy["far"], sz["far"]
    )
    az_mate, sx_mate, cy_mate = small = [send(v, n, "c") for v in (az[n], sx[n], cy)]
    axz, sxz = {}, {}
    axz[n] = send(axxy[n], n, "z")
    sxz[n] = send(sz[n], n, "x")
    axz["far"] = send(after(axxy["far"], *small), "far", "z")
    sxz["far"] = send(after(sz["far"], *small), "far", "x")
    four_mate = send(after(four, *small), n, "c")
    cxy = send(after(cx, cy, four_mate), n, "y")

    def blocks_of(g):
        act = {"": (a0x[g], 0, 0), "x": (a0x[g], 1, 0), "y": (ay[g], 0, 0), "xy": (ay[g], 1, 0)}
        act |= {"z": (az[g], 0, 0), "yz": (az[g], 1, 0), "xz": (axz[g], 0, 0), "xyz": (axz[g], 1, 0)}
        sig = {"": (s0y[g], 0, 0), "y": (s0y[g], 1, 0), "z": (sz[g], 0, 0), "yz": (sz[g], 1, 0)}
        sig |= {"x": (sx[g], 0, 0), "xy": (sx[g], 1, 0), "xz": (sxz[g], 0, 0), "xyz": (sxz[g], 1, 0)}
        return act, sig

    act, sig = blocks_of("far")
    right = {k: (act[k], sig[k]) for k in act}
    act, sig = blocks_of("near")
    coef = {"": (c0z, 0, 0), "z": (c0z, 1, 0), "x": (cx, 0, 0), "xz": (cx, 1, 0)}
    coef |= {"y": (cy, 0, 0), "yz": (cy, 1, 0), "xy": (cxy, 0, 0), "xyz": (cxy, 1, 0)}
    left = {k: (act[k], sig[k], coef[k]) for k in act}
    right_1 = [right[k] for k in ("xy", "yz", "x", "y", "z", "")]
    right_2 = [right[k] for k in ("xz", "xyz")]
    first, second = ("", "x", "y", "z", "yz"), ("xy", "xz", "xyz")

    coef[""] = (after(c0z, *small), 0, 0)
    act_mate = {"": (four_mate, 0, 0), "x": (four_mate, 1, 0), "y": (four_mate, 2, 0), "xy": (four_mate, 3, 0)}
    act_mate |= {"z": (az_mate, 0, 0), "yz": (az_mate, 1, 0)}
    sig_mate = {"": (four_mate, 0, 1), "y": (four_mate, 1, 1), "z": (four_mate, 2, 1), "yz": (four_mate, 3, 1)}
    sig_mate |= {"x": (sx_mate, 0, 0), "xy": (sx_mate, 1, 0)}
    coef_mate = {"": (four_mate, 0, 2), "z": (four_mate, 1, 2), "x": (four_mate, 2, 2), "xz": (four_mate, 3, 2)}
    coef_mate |= {"y": (cy_mate, 0, 0), "yz": (cy_mate, 1, 0)}
    left_1 = [(left[k][0], left[k][1], coef[k]) for k in first]
    left_1 += [(act_mate[k], sig_mate[k], coef_mate[k]) for k in first]
    (total_1,), (rows_1, coefs_1, wide_1) = partial_sums([(right_1, 0, 960, None, 0)], left_1, False, "early")
    axz_mate, sxz_mate = [send(after(v, total_1), n, "c") for v in (axz[n], sxz[n])]
    cxy_mate = send(cxy, n, "c")
    (total_2,), (wide_2,) = partial_sums(
        [(right_2, 0, 320, None, 0)], (after(rows_1, total_1), coefs_1), False, "early_right"
    )
    act_mate |= {"xz": (axz_mate, 0, 0), "xyz": (axz_mate, 1, 0)}
    sig_mate |= {"xz": (sxz_mate, 0, 0), "xyz": (sxz_mate, 1, 0)}
    coef_mate |= {"xy": (cxy_mate, 0, 0), "xyz": (cxy_mate, 1, 0)}
    left_2 = [left[k] for k in second]
    left_2 += [(act_mate[k], sig_mate[k], coef_mate[k]) for k in second]

    (sum_xz, sum_xyz, sum_xy, sum_yz), (rows_2, coefs_2) = partial_sums(
        [(wide_2, 0, 320, total_2, 0), (wide_1, 0, 320, total_1, 0)], left_2, True, "second_far"
    )
    part_x, part_y, part_z = send(sum_xz, "far", "z"), send(sum_xy, "far", "x"), send(sum_yz, "far", "y")
    got_xyz = send(sum_xyz, "far", "xyz")
    (sum_x, sum_y, sum_z, own), _ = partial_sums(
        [(wide_1, 320, 640, total_1, 320)], (after(rows_2, sum_xz), coefs_2), True, "second_near"
    )
    got_x = send(after(sum_x + part_x, own), "far", "x")
    got_y = send(after(sum_y + part_y, own), "far", "y")
    got_z = send(after(sum_z + part_z, own), "far", "z")

    product = own + got_xyz + got_x + got_y + got_z
    product = product * (1.0 / (FEAT * FEAT))
    classes = jnp.arange(CLASSES, dtype=jnp.int32)
    targets = (labels[:, None] == classes[None, :]).astype(f32) - 1.0 / CLASSES
    return (coefs + damping * (targets - product - ridge * coefs)).T


def solution(mesh):
    in_specs = (P(AXES, None), P(AXES, None), P(AXES), P(None, AXES))
    return jax.shard_map(shards, mesh=mesh, in_specs=in_specs, out_specs=P(None, AXES), check_vma=False)
```

```python
import functools

import jax
import jax.numpy as jnp
from jax import lax
from jax.experimental import pallas as pl
from jax.experimental.pallas import tpu as pltpu
from jax.sharding import PartitionSpec as P

FEAT = 768
CLASSES = 345
LANES = 384
OWN = 160
AXES = ("row", "col")

damping = 0.8
ridge = 0.1

f32, bf16 = jnp.float32, jnp.bfloat16
NT = (((1,), (1,)), ((), ()))
NN = (((1,), (0,)), ((), ()))
VMEM = pl.BlockSpec(memory_space=pltpu.VMEM)


def encode(x, y, z, core):
    return ((((z >> 1) * 4 + x) * 4 + y) * 2 + (z & 1)) * 2 + core


def decode(index):
    return (index >> 4) & 3, (index >> 2) & 3, (index >> 6) * 2 + ((index >> 1) & 1), index & 1


def moves(group, dims):
    pairs = []
    for index in range(128):
        x, y, z, core = decode(index)
        place = {"x": x, "y": y, "z": z}
        for dim in dims:
            if dim == "c":
                core ^= 1
            else:
                place[dim] = 3 - place[dim] if group == "far" else place[dim] ^ 1
        pairs.append((index, encode(place["x"], place["y"], place["z"], core)))
    return pairs


def send(value, group, dims):
    return lax.ppermute(value, AXES, moves(group, dims))


def after(value, *others):
    return lax.optimization_barrier((value, *others))[0]


def dot(a, b, dims):
    return lax.dot_general(a, b, dims, preferred_element_type=f32)


def split_kernel(coef, split):
    split[...] = jnp.zeros_like(split)
    values = coef[...]
    high = values.astype(bf16)
    split[:, :CLASSES] = high
    split[:, LANES : LANES + CLASSES] = (values - high.astype(f32)).astype(bf16)


def split_coefs(coefs):
    return pl.pallas_call(
        split_kernel,
        out_shape=pltpu.VMEM((OWN, 2 * LANES), bf16),
        in_specs=[VMEM],
        out_specs=VMEM,
        compiler_params=pltpu.CompilerParams(vmem_limit_bytes=4 << 20),
        name="split_coefs",
    )(coefs)


def arrange_kernel(plan, n_in, *refs):
    for out, pieces in zip(refs[n_in:], plan):
        for source, row, out_row, out_col in pieces:
            out[out_row * OWN : (out_row + 1) * OWN, out_col * FEAT : (out_col + 1) * FEAT] = refs[source][
                row * OWN : (row + 1) * OWN, :
            ]


def arrange(outputs, name):
    arrays, plan, shapes = [], [], []

    def place(array):
        for i, known in enumerate(arrays):
            if known is array:
                return i
        arrays.append(array)
        return len(arrays) - 1

    for columns in outputs:
        plan.append(
            [
                (place(array), block, out_row, out_col)
                for out_col, column in enumerate(columns)
                for out_row, (array, block) in enumerate(column)
            ]
        )
        shapes.append(pltpu.VMEM((len(columns[0]) * OWN, len(columns) * FEAT), bf16))
    return pl.pallas_call(
        functools.partial(arrange_kernel, plan, len(arrays)),
        out_shape=shapes,
        in_specs=[VMEM] * len(arrays),
        out_specs=[VMEM] * len(shapes),
        compiler_params=pltpu.CompilerParams(vmem_limit_bytes=8 << 20),
        name=name,
    )(*arrays)


def block_rows(count):
    return 480 if count % 480 == 0 else count


def block_kernel(plan, n_in, parts, left_ready, apart, *refs):
    refs, (high, low) = refs[:-2], refs[-2:]
    inputs, refs = refs[:n_in], refs[n_in:]
    if left_ready:
        (left, split), refs = refs[:2], refs[2:]
    rights, totals = [None] * len(parts), [None] * len(parts)
    for i, (ready, _, _, total_row) in enumerate(parts):
        if ready:
            rights[i], refs = refs[0], refs[1:]
        if total_row is not None:
            totals[i], refs = refs[0], refs[1:]
    n_outs = sum(part[2] for part in parts) // OWN if apart else len(parts)
    outs, refs = refs[:n_outs], refs[n_outs:]
    if not left_ready:
        (left, split), refs = refs[:2], refs[2:]
    for i, (ready, _, _, _) in enumerate(parts):
        if not ready:
            rights[i], refs = refs[0], refs[1:]
    targets = (left, split, *rights)
    for target, out_row, out_col, source, row, col in plan:
        targets[target][out_row * OWN : (out_row + 1) * OWN, out_col * FEAT : (out_col + 1) * FEAT] = inputs[source][
            row * OWN : (row + 1) * OWN, col * FEAT : (col + 1) * FEAT
        ]
    done = 0
    for i, (_, first, count, total_row) in enumerate(parts):
        right = rights[i]
        rows = block_rows(count)
        for start in range(0, count, rows):
            n = slice(first + start, first + start + rows)
            for at in range(0, left.shape[0], 512):
                m = slice(at, min(at + 512, left.shape[0]))
                gram_a = dot(right[n, :FEAT], left[m, :FEAT], NT)
                gram_s = dot(right[n, FEAT:], left[m, FEAT:], NT)
                kernel = gram_a * gram_s
                rounded = kernel.astype(bf16)
                high[:rows, m] = rounded
                low[:rows, m] = (kernel - rounded.astype(f32)).astype(bf16)
            both = dot(high[:rows, :], split[...], NN)
            part = both[:, :LANES] + both[:, LANES:] + dot(low[:rows, :], split[:, :LANES], NN)
            if total_row is not None:
                part = part + totals[i][total_row + start : total_row + start + rows, :]
            if apart:
                for k in range(rows // OWN):
                    outs[done + k][...] = part[k * OWN : (k + 1) * OWN, :CLASSES]
                done += rows // OWN
            else:
                outs[i][start : start + rows, :] = part


def partial_sums(rights, left, apart, name):
    arrays, plan = [], []

    def place(array):
        for i, known in enumerate(arrays):
            if known is array:
                return i
        arrays.append(array)
        return len(arrays) - 1

    left_ready = isinstance(left, tuple)
    if not left_ready:
        for i, (act, sig, coef) in enumerate(left):
            plan.append((0, i, 0, place(act[0]), act[1], act[2]))
            plan.append((0, i, 1, place(sig[0]), sig[1], sig[2]))
            plan.append((1, i, 0, place(coef[0]), coef[1], coef[2]))
    for target, (blocks, *_) in enumerate(rights):
        if isinstance(blocks, list):
            for i, (act, sig) in enumerate(blocks):
                plan.append((2 + target, i, 0, place(act[0]), act[1], act[2]))
                plan.append((2 + target, i, 1, place(sig[0]), sig[1], sig[2]))
    n_in = len(arrays)
    left_rows = left[0].shape[0] if left_ready else len(left) * OWN
    if left_ready:
        arrays += left
    parts, laid = [], []
    for blocks, first, count, total, total_row in rights:
        ready = not isinstance(blocks, list)
        parts.append((ready, first, count, None if total is None else total_row))
        if ready:
            arrays.append(blocks)
        else:
            laid.append(pltpu.VMEM((len(blocks) * OWN, 2 * FEAT), bf16))
        if total is not None:
            arrays.append(total)
    if not left_ready:
        laid = [pltpu.VMEM((left_rows, 2 * FEAT), bf16), pltpu.VMEM((left_rows, 2 * LANES), bf16)] + laid
    if apart:
        sums = [pltpu.VMEM((OWN, CLASSES), f32)] * (sum(part[2] for part in parts) // OWN)
    else:
        sums = [pltpu.VMEM((part[2], LANES), f32) for part in parts]
    outs = pl.pallas_call(
        functools.partial(block_kernel, plan, n_in, parts, left_ready, apart),
        out_shape=sums + laid,
        in_specs=[VMEM] * len(arrays),
        out_specs=[VMEM] * (len(sums) + len(laid)),
        scratch_shapes=[pltpu.VMEM((max(block_rows(part[2]) for part in parts), left_rows), bf16)] * 2,
        cost_estimate=pl.CostEstimate(
            flops=sum(part[2] for part in parts) * left_rows * 5400, bytes_accessed=1_000_000, transcendentals=0
        ),
        compiler_params=pltpu.CompilerParams(vmem_limit_bytes=16 << 20),
        name=name,
    )(*arrays)
    return outs[: len(sums)], outs[len(sums) :]


def shards(activations, signals, labels, coefficients):
    coefs = coefficients.T
    groups = ("far", "near")
    a, s, c = {}, {}, {}
    for g in groups:
        a[g, "x"] = send(activations, g, "x")
        s[g, "y"] = send(signals, g, "y")
    c0 = split_coefs(coefs)
    cz = send(c0, "near", "z")
    act_own, sig_own = arrange([[[(after(v, c0), 0)]] for v in (activations, signals)], "own_rows")

    def together(*values):
        return lax.optimization_barrier(values)

    a["far", "x"], a["near", "x"], s["far", "y"], s["near", "y"], cz = together(
        a["far", "x"], a["near", "x"], s["far", "y"], s["near", "y"], cz
    )

    pairs = arrange(
        [[[(act_own, 0), (a[g, "x"], 0)]] for g in groups]
        + [[[(sig_own, 0), (s[g, "y"], 0)]] for g in groups]
        + [[[(c0, 0), (cz, 0)]]],
        "pairs",
    )
    a0x, s0y, c0z = dict(zip(groups, pairs[:2])), dict(zip(groups, pairs[2:4])), pairs[4]
    ay, sz = {}, {}
    for g in groups:
        ay[g] = send(a0x[g], g, "y")
        sz[g] = send(s0y[g], g, "z")
    cx = send(c0z, "near", "x")
    ay["far"], ay["near"], sz["far"], sz["near"], cx = together(ay["far"], ay["near"], sz["far"], sz["near"], cx)
    turned = arrange(
        [[[(a0x[g], k), (ay[g], k)]] for k in (0, 1) for g in groups],
        "turn",
    )
    a0y, axxy = dict(zip(groups, turned[:2])), dict(zip(groups, turned[2:]))
    az, sx = {}, {}
    for g in groups:
        sx[g] = send(after(s0y[g], sz[g]), g, "x")
    cy = send(after(c0z, cx), "near", "y")
    for g in groups:
        az[g] = send(a0y[g], g, "z")
    n = "near"
    (four,) = arrange(
        [
            [
                [(a0x[n], 0), (a0x[n], 1), (ay[n], 0), (ay[n], 1)],
                [(s0y[n], 0), (s0y[n], 1), (sz[n], 0), (sz[n], 1)],
                [(c0z, 0), (c0z, 1), (cx, 0), (cx, 1)],
            ]
        ],
        "four",
    )
    az["far"], az[n], sx["far"], sx[n], cy, four, axxy[n], sz[n], axxy["far"], sz["far"] = together(
        az["far"], az[n], sx["far"], sx[n], cy, four, axxy[n], sz[n], axxy["far"], sz["far"]
    )
    az_mate, sx_mate, cy_mate = small = [send(v, n, "c") for v in (az[n], sx[n], cy)]
    axz, sxz = {}, {}
    axz[n] = send(axxy[n], n, "z")
    sxz[n] = send(sz[n], n, "x")

    sxz["far"] = send(after(sz["far"], *small), "far", "x")
    four_mate = send(after(four, *small), n, "c")
    cxy = send(after(cx, *small), n, "y")
    axz["far"] = send(after(axxy["far"], four_mate), "far", "z")

    def blocks_of(g):
        act = {"": (a0x[g], 0, 0), "x": (a0x[g], 1, 0), "y": (ay[g], 0, 0), "xy": (ay[g], 1, 0)}
        act |= {"z": (az[g], 0, 0), "yz": (az[g], 1, 0), "xz": (axz[g], 0, 0), "xyz": (axz[g], 1, 0)}
        sig = {"": (s0y[g], 0, 0), "y": (s0y[g], 1, 0), "z": (sz[g], 0, 0), "yz": (sz[g], 1, 0)}
        sig |= {"x": (sx[g], 0, 0), "xy": (sx[g], 1, 0), "xz": (sxz[g], 0, 0), "xyz": (sxz[g], 1, 0)}
        return act, sig

    act, sig = blocks_of("far")
    right = {k: (act[k], sig[k]) for k in act}
    act, sig = blocks_of("near")
    coef = {"": (c0z, 0, 0), "z": (c0z, 1, 0), "x": (cx, 0, 0), "xz": (cx, 1, 0)}
    coef |= {"y": (cy, 0, 0), "yz": (cy, 1, 0), "xy": (cxy, 0, 0), "xyz": (cxy, 1, 0)}
    left = {k: (act[k], sig[k], coef[k]) for k in act}
    right_1 = [right[k] for k in ("xy", "yz", "x", "y", "z", "")]
    right_2 = [right[k] for k in ("xz", "xyz")]
    first, second = ("", "x", "y", "z", "yz"), ("xy", "xz", "xyz")

    coef[""] = (after(c0z, *small), 0, 0)
    act_mate = {"": (four_mate, 0, 0), "x": (four_mate, 1, 0), "y": (four_mate, 2, 0), "xy": (four_mate, 3, 0)}
    act_mate |= {"z": (az_mate, 0, 0), "yz": (az_mate, 1, 0)}
    sig_mate = {"": (four_mate, 0, 1), "y": (four_mate, 1, 1), "z": (four_mate, 2, 1), "yz": (four_mate, 3, 1)}
    sig_mate |= {"x": (sx_mate, 0, 0), "xy": (sx_mate, 1, 0)}
    coef_mate = {"": (four_mate, 0, 2), "z": (four_mate, 1, 2), "x": (four_mate, 2, 2), "xz": (four_mate, 3, 2)}
    coef_mate |= {"y": (cy_mate, 0, 0), "yz": (cy_mate, 1, 0)}
    left_1 = [(left[k][0], left[k][1], coef[k]) for k in first]
    left_1 += [(act_mate[k], sig_mate[k], coef_mate[k]) for k in first]
    (total_1,), (rows_1, coefs_1, wide_1) = partial_sums([(right_1, 0, 960, None, 0)], left_1, False, "early")
    axz_mate, sxz_mate = [send(after(v, total_1), n, "c") for v in (axz[n], sxz[n])]
    cxy_mate = send(after(cxy, total_1), n, "c")
    (total_2,), (wide_2,) = partial_sums(
        [(right_2, 0, 320, None, 0)], (after(rows_1, total_1), coefs_1), False, "early_right"
    )
    act_mate |= {"xz": (axz_mate, 0, 0), "xyz": (axz_mate, 1, 0)}
    sig_mate |= {"xz": (sxz_mate, 0, 0), "xyz": (sxz_mate, 1, 0)}
    coef_mate |= {"xy": (cxy_mate, 0, 0), "xyz": (cxy_mate, 1, 0)}
    left_2 = [left[k] for k in second]
    left_2 += [(act_mate[k], sig_mate[k], coef_mate[k]) for k in second]

    (sum_xz, sum_xyz, sum_xy, sum_yz), (rows_2, coefs_2) = partial_sums(
        [(wide_2, 0, 320, total_2, 0), (wide_1, 0, 320, total_1, 0)], left_2, True, "second_far"
    )
    part_x, part_y, part_z = send(sum_xz, "far", "z"), send(sum_xy, "far", "x"), send(sum_yz, "far", "y")
    got_xyz = send(sum_xyz, "far", "xyz")
    (sum_x, sum_y, sum_z, own), _ = partial_sums(
        [(wide_1, 320, 640, total_1, 320)], (after(rows_2, sum_xz), coefs_2), True, "second_near"
    )
    got_x = send(after(sum_x + part_x, own), "far", "x")
    got_y = send(after(sum_y + part_y, own), "far", "y")
    got_z = send(after(sum_z + part_z, own), "far", "z")

    product = own + got_xyz + got_x + got_y + got_z
    product = product * (1.0 / (FEAT * FEAT))
    classes = jnp.arange(CLASSES, dtype=jnp.int32)
    targets = (labels[:, None] == classes[None, :]).astype(f32) - 1.0 / CLASSES
    return (coefs + damping * (targets - product - ridge * coefs)).T


def solution(mesh):
    in_specs = (P(AXES, None), P(AXES, None), P(AXES), P(None, AXES))
    return jax.shard_map(shards, mesh=mesh, in_specs=in_specs, out_specs=P(None, AXES), check_vma=False)
```

```python
import functools

import jax
import jax.numpy as jnp
from jax import lax
from jax.experimental import pallas as pl
from jax.experimental.pallas import tpu as pltpu
from jax.sharding import PartitionSpec as P

FEAT = 768
CLASSES = 345
LANES = 384
OWN = 160
AXES = ("row", "col")

damping = 0.8
ridge = 0.1

f32, bf16 = jnp.float32, jnp.bfloat16
NT = (((1,), (1,)), ((), ()))
NN = (((1,), (0,)), ((), ()))
VMEM = pl.BlockSpec(memory_space=pltpu.VMEM)


def encode(x, y, z, core):
    return ((((z >> 1) * 4 + x) * 4 + y) * 2 + (z & 1)) * 2 + core


def decode(index):
    return (index >> 4) & 3, (index >> 2) & 3, (index >> 6) * 2 + ((index >> 1) & 1), index & 1


def moves(group, dims):
    pairs = []
    for index in range(128):
        x, y, z, core = decode(index)
        place = {"x": x, "y": y, "z": z}
        for dim in dims:
            if dim == "c":
                core ^= 1
            else:
                place[dim] = 3 - place[dim] if group == "far" else place[dim] ^ 1
        pairs.append((index, encode(place["x"], place["y"], place["z"], core)))
    return pairs


def send(value, group, dims):
    return lax.ppermute(value, AXES, moves(group, dims))


def after(value, *others):
    return lax.optimization_barrier((value, *others))[0]


def dot(a, b, dims):
    return lax.dot_general(a, b, dims, preferred_element_type=f32)


def split_kernel(coef, split):
    split[...] = jnp.zeros_like(split)
    values = coef[...]
    high = values.astype(bf16)
    split[:, :CLASSES] = high
    split[:, LANES : LANES + CLASSES] = (values - high.astype(f32)).astype(bf16)


def split_coefs(coefs):
    return pl.pallas_call(
        split_kernel,
        out_shape=pltpu.VMEM((OWN, 2 * LANES), bf16),
        in_specs=[VMEM],
        out_specs=VMEM,
        compiler_params=pltpu.CompilerParams(vmem_limit_bytes=4 << 20),
        name="split_coefs",
    )(coefs)


def arrange_kernel(plan, n_in, *refs):
    for out, pieces in zip(refs[n_in:], plan):
        for source, row, out_row, out_col in pieces:
            out[out_row * OWN : (out_row + 1) * OWN, out_col * FEAT : (out_col + 1) * FEAT] = refs[source][
                row * OWN : (row + 1) * OWN, :
            ]


def arrange(outputs, name):
    arrays, plan, shapes = [], [], []

    def place(array):
        for i, known in enumerate(arrays):
            if known is array:
                return i
        arrays.append(array)
        return len(arrays) - 1

    for columns in outputs:
        plan.append(
            [
                (place(array), block, out_row, out_col)
                for out_col, column in enumerate(columns)
                for out_row, (array, block) in enumerate(column)
            ]
        )
        shapes.append(pltpu.VMEM((len(columns[0]) * OWN, len(columns) * FEAT), bf16))
    return pl.pallas_call(
        functools.partial(arrange_kernel, plan, len(arrays)),
        out_shape=shapes,
        in_specs=[VMEM] * len(arrays),
        out_specs=[VMEM] * len(shapes),
        compiler_params=pltpu.CompilerParams(vmem_limit_bytes=8 << 20),
        name=name,
    )(*arrays)


def block_rows(count):
    return 480 if count % 480 == 0 else count


def block_kernel(plan, n_in, parts, left_ready, apart, *refs):
    refs, (high, low) = refs[:-2], refs[-2:]
    inputs, refs = refs[:n_in], refs[n_in:]
    if left_ready:
        (left, split), refs = refs[:2], refs[2:]
    rights, totals = [None] * len(parts), [None] * len(parts)
    for i, (ready, _, _, total_row) in enumerate(parts):
        if ready:
            rights[i], refs = refs[0], refs[1:]
        if total_row is not None:
            totals[i], refs = refs[0], refs[1:]
    n_outs = sum(part[2] for part in parts) // OWN if apart else len(parts)
    outs, refs = refs[:n_outs], refs[n_outs:]
    if not left_ready:
        (left, split), refs = refs[:2], refs[2:]
    for i, (ready, _, _, _) in enumerate(parts):
        if not ready:
            rights[i], refs = refs[0], refs[1:]
    targets = (left, split, *rights)
    for target, out_row, out_col, source, row, col in plan:
        targets[target][out_row * OWN : (out_row + 1) * OWN, out_col * FEAT : (out_col + 1) * FEAT] = inputs[source][
            row * OWN : (row + 1) * OWN, col * FEAT : (col + 1) * FEAT
        ]
    done = 0
    for i, (_, first, count, total_row) in enumerate(parts):
        right = rights[i]
        rows = block_rows(count)
        for start in range(0, count, rows):
            n = slice(first + start, first + start + rows)
            for at in range(0, left.shape[0], 512):
                m = slice(at, min(at + 512, left.shape[0]))
                gram_a = dot(right[n, :FEAT], left[m, :FEAT], NT)
                gram_s = dot(right[n, FEAT:], left[m, FEAT:], NT)
                kernel = gram_a * gram_s
                rounded = kernel.astype(bf16)
                high[:rows, m] = rounded
                low[:rows, m] = (kernel - rounded.astype(f32)).astype(bf16)
            both = dot(high[:rows, :], split[...], NN)
            part = both[:, :LANES] + both[:, LANES:] + dot(low[:rows, :], split[:, :LANES], NN)
            if total_row is not None:
                part = part + totals[i][total_row + start : total_row + start + rows, :]
            if apart:
                for k in range(rows // OWN):
                    outs[done + k][...] = part[k * OWN : (k + 1) * OWN, :CLASSES]
                done += rows // OWN
            else:
                outs[i][start : start + rows, :] = part


def partial_sums(rights, left, apart, name):
    arrays, plan = [], []

    def place(array):
        for i, known in enumerate(arrays):
            if known is array:
                return i
        arrays.append(array)
        return len(arrays) - 1

    left_ready = isinstance(left, tuple)
    if not left_ready:
        for i, (act, sig, coef) in enumerate(left):
            plan.append((0, i, 0, place(act[0]), act[1], act[2]))
            plan.append((0, i, 1, place(sig[0]), sig[1], sig[2]))
            plan.append((1, i, 0, place(coef[0]), coef[1], coef[2]))
    for target, (blocks, *_) in enumerate(rights):
        if isinstance(blocks, list):
            for i, (act, sig) in enumerate(blocks):
                plan.append((2 + target, i, 0, place(act[0]), act[1], act[2]))
                plan.append((2 + target, i, 1, place(sig[0]), sig[1], sig[2]))
    n_in = len(arrays)
    left_rows = left[0].shape[0] if left_ready else len(left) * OWN
    if left_ready:
        arrays += left
    parts, laid = [], []
    for blocks, first, count, total, total_row in rights:
        ready = not isinstance(blocks, list)
        parts.append((ready, first, count, None if total is None else total_row))
        if ready:
            arrays.append(blocks)
        else:
            laid.append(pltpu.VMEM((len(blocks) * OWN, 2 * FEAT), bf16))
        if total is not None:
            arrays.append(total)
    if not left_ready:
        laid = [pltpu.VMEM((left_rows, 2 * FEAT), bf16), pltpu.VMEM((left_rows, 2 * LANES), bf16)] + laid
    if apart:
        sums = [pltpu.VMEM((OWN, CLASSES), f32)] * (sum(part[2] for part in parts) // OWN)
    else:
        sums = [pltpu.VMEM((part[2], LANES), f32) for part in parts]
    outs = pl.pallas_call(
        functools.partial(block_kernel, plan, n_in, parts, left_ready, apart),
        out_shape=sums + laid,
        in_specs=[VMEM] * len(arrays),
        out_specs=[VMEM] * (len(sums) + len(laid)),
        scratch_shapes=[pltpu.VMEM((max(block_rows(part[2]) for part in parts), left_rows), bf16)] * 2,
        cost_estimate=pl.CostEstimate(
            flops=sum(part[2] for part in parts) * left_rows * 5400, bytes_accessed=1_000_000, transcendentals=0
        ),
        compiler_params=pltpu.CompilerParams(vmem_limit_bytes=16 << 20),
        name=name,
    )(*arrays)
    return outs[: len(sums)], outs[len(sums) :]


def shards(activations, signals, labels, coefficients):
    coefs = coefficients.T
    groups = ("far", "near")
    a, s, c = {}, {}, {}
    for g in groups:
        a[g, "x"] = send(activations, g, "x")
        s[g, "y"] = send(signals, g, "y")
    c0 = split_coefs(coefs)
    cz = send(c0, "near", "z")
    act_own, sig_own = arrange([[[(after(v, c0), 0)]] for v in (activations, signals)], "own_rows")

    def together(*values):
        return lax.optimization_barrier(values)

    a["far", "x"], a["near", "x"], s["far", "y"], s["near", "y"], cz = together(
        a["far", "x"], a["near", "x"], s["far", "y"], s["near", "y"], cz
    )

    pairs = arrange(
        [[[(act_own, 0), (a[g, "x"], 0)]] for g in groups]
        + [[[(sig_own, 0), (s[g, "y"], 0)]] for g in groups]
        + [[[(c0, 0), (cz, 0)]]],
        "pairs",
    )
    a0x, s0y, c0z = dict(zip(groups, pairs[:2])), dict(zip(groups, pairs[2:4])), pairs[4]
    ay, sz = {}, {}
    for g in groups:
        ay[g] = send(a0x[g], g, "y")
        sz[g] = send(s0y[g], g, "z")
    cx = send(c0z, "near", "x")
    ay["far"], ay["near"], sz["far"], sz["near"], cx = together(ay["far"], ay["near"], sz["far"], sz["near"], cx)
    turned = arrange(
        [[[(a0x[g], k), (ay[g], k)]] for k in (0, 1) for g in groups],
        "turn",
    )
    a0y, axxy = dict(zip(groups, turned[:2])), dict(zip(groups, turned[2:]))
    az, sx = {}, {}
    for g in groups:
        sx[g] = send(after(s0y[g], sz[g]), g, "x")
    cy = send(after(c0z, cx), "near", "y")
    for g in groups:
        az[g] = send(a0y[g], g, "z")
    n = "near"
    (four,) = arrange(
        [
            [
                [(a0x[n], 0), (a0x[n], 1), (ay[n], 0), (ay[n], 1)],
                [(s0y[n], 0), (s0y[n], 1), (sz[n], 0), (sz[n], 1)],
                [(c0z, 0), (c0z, 1), (cx, 0), (cx, 1)],
            ]
        ],
        "four",
    )
    az["far"], az[n], sx["far"], sx[n], cy, four, axxy[n], sz[n], axxy["far"], sz["far"] = together(
        az["far"], az[n], sx["far"], sx[n], cy, four, axxy[n], sz[n], axxy["far"], sz["far"]
    )
    az_mate, sx_mate, cy_mate = small = [send(v, n, "c") for v in (az[n], sx[n], cy)]
    axz, sxz = {}, {}
    axz[n] = send(axxy[n], n, "z")
    sxz[n] = send(sz[n], n, "x")

    sxz["far"] = send(after(sz["far"], *small), "far", "x")
    four_mate = send(after(four, *small), n, "c")
    cxy = send(after(cx, *small), n, "y")
    axz["far"] = send(after(axxy["far"], four_mate), "far", "z")

    def blocks_of(g):
        act = {"": (a0x[g], 0, 0), "x": (a0x[g], 1, 0), "y": (ay[g], 0, 0), "xy": (ay[g], 1, 0)}
        act |= {"z": (az[g], 0, 0), "yz": (az[g], 1, 0), "xz": (axz[g], 0, 0), "xyz": (axz[g], 1, 0)}
        sig = {"": (s0y[g], 0, 0), "y": (s0y[g], 1, 0), "z": (sz[g], 0, 0), "yz": (sz[g], 1, 0)}
        sig |= {"x": (sx[g], 0, 0), "xy": (sx[g], 1, 0), "xz": (sxz[g], 0, 0), "xyz": (sxz[g], 1, 0)}
        return act, sig

    act, sig = blocks_of("far")
    right = {k: (act[k], sig[k]) for k in act}
    act, sig = blocks_of("near")
    coef = {"": (c0z, 0, 0), "z": (c0z, 1, 0), "x": (cx, 0, 0), "xz": (cx, 1, 0)}
    coef |= {"y": (cy, 0, 0), "yz": (cy, 1, 0), "xy": (cxy, 0, 0), "xyz": (cxy, 1, 0)}
    left = {k: (act[k], sig[k], coef[k]) for k in act}
    right_1 = [right[k] for k in ("xy", "yz", "x", "y", "z", "")]
    right_2 = [right[k] for k in ("xz", "xyz")]
    first, second = ("", "x", "y", "z", "yz"), ("xy", "xz", "xyz")

    coef[""] = (after(c0z, *small), 0, 0)
    act_mate = {"": (four_mate, 0, 0), "x": (four_mate, 1, 0), "y": (four_mate, 2, 0), "xy": (four_mate, 3, 0)}
    act_mate |= {"z": (az_mate, 0, 0), "yz": (az_mate, 1, 0)}
    sig_mate = {"": (four_mate, 0, 1), "y": (four_mate, 1, 1), "z": (four_mate, 2, 1), "yz": (four_mate, 3, 1)}
    sig_mate |= {"x": (sx_mate, 0, 0), "xy": (sx_mate, 1, 0)}
    coef_mate = {"": (four_mate, 0, 2), "z": (four_mate, 1, 2), "x": (four_mate, 2, 2), "xz": (four_mate, 3, 2)}
    coef_mate |= {"y": (cy_mate, 0, 0), "yz": (cy_mate, 1, 0)}
    left_1 = [(left[k][0], left[k][1], coef[k]) for k in first]
    left_1 += [(act_mate[k], sig_mate[k], coef_mate[k]) for k in first]
    (total_1,), (rows_1, coefs_1, wide_1) = partial_sums([(right_1, 0, 960, None, 0)], left_1, False, "early")
    axz_mate, sxz_mate = [send(after(v, total_1), n, "c") for v in (axz[n], sxz[n])]
    cxy_mate = send(after(cxy, total_1), n, "c")
    (total_2,), (wide_2,) = partial_sums(
        [(right_2, 0, 320, None, 0)], (after(rows_1, total_1), coefs_1), False, "early_right"
    )
    act_mate |= {"xz": (axz_mate, 0, 0), "xyz": (axz_mate, 1, 0)}
    sig_mate |= {"xz": (sxz_mate, 0, 0), "xyz": (sxz_mate, 1, 0)}
    coef_mate |= {"xy": (cxy_mate, 0, 0), "xyz": (cxy_mate, 1, 0)}
    left_2 = [left[k] for k in second]
    left_2 += [(act_mate[k], sig_mate[k], coef_mate[k]) for k in second]

    (sum_xz, sum_xyz, sum_xy, sum_yz), (rows_2, coefs_2) = partial_sums(
        [(wide_2, 0, 320, total_2, 0), (wide_1, 0, 320, total_1, 0)], left_2, True, "second_far"
    )
    part_x, part_y, part_z = send(sum_xz, "far", "z"), send(sum_xy, "far", "x"), send(sum_yz, "far", "y")
    got_xyz = send(sum_xyz, "far", "xyz")
    (sum_x, sum_y, sum_z), _ = partial_sums(
        [(wide_1, 320, 480, total_1, 320)], (after(rows_2, sum_xz), coefs_2), True, "second_near"
    )
    got_x = send(after(sum_x + part_x, sum_z), "far", "x")
    got_y = send(after(sum_y + part_y, sum_z), "far", "y")
    last = sum_z + part_z
    got_z = send(last, "far", "z")
    (own,), _ = partial_sums([(wide_1, 800, 160, total_1, 800)], (after(rows_2, last), coefs_2), True, "second_here")

    product = own + got_xyz + got_x + got_y + got_z
    product = product * (1.0 / (FEAT * FEAT))
    classes = jnp.arange(CLASSES, dtype=jnp.int32)
    targets = (labels[:, None] == classes[None, :]).astype(f32) - 1.0 / CLASSES
    return (coefs + damping * (targets - product - ridge * coefs)).T


def solution(mesh):
    in_specs = (P(AXES, None), P(AXES, None), P(AXES), P(None, AXES))
    return jax.shard_map(shards, mesh=mesh, in_specs=in_specs, out_specs=P(None, AXES), check_vma=False)
```

```python
import functools

import jax
import jax.numpy as jnp
from jax import lax
from jax.experimental import pallas as pl
from jax.experimental.pallas import tpu as pltpu
from jax.sharding import PartitionSpec as P

FEAT = 768
CLASSES = 345
LANES = 384
OWN = 160
AXES = ("row", "col")

damping = 0.8
ridge = 0.1

f32, bf16 = jnp.float32, jnp.bfloat16
NT = (((1,), (1,)), ((), ()))
NN = (((1,), (0,)), ((), ()))
VMEM = pl.BlockSpec(memory_space=pltpu.VMEM)


def encode(x, y, z, core):
    return ((((z >> 1) * 4 + x) * 4 + y) * 2 + (z & 1)) * 2 + core


def decode(index):
    return (index >> 4) & 3, (index >> 2) & 3, (index >> 6) * 2 + ((index >> 1) & 1), index & 1


def moves(group, dims):
    pairs = []
    for index in range(128):
        x, y, z, core = decode(index)
        place = {"x": x, "y": y, "z": z}
        for dim in dims:
            if dim == "c":
                core ^= 1
            else:
                place[dim] = 3 - place[dim] if group == "far" else place[dim] ^ 1
        pairs.append((index, encode(place["x"], place["y"], place["z"], core)))
    return pairs


def send(value, group, dims):
    return lax.ppermute(value, AXES, moves(group, dims))


def after(value, *others):
    return lax.optimization_barrier((value, *others))[0]


def dot(a, b, dims):
    return lax.dot_general(a, b, dims, preferred_element_type=f32)


def split_kernel(coef, split):
    split[...] = jnp.zeros_like(split)
    values = coef[...]
    high = values.astype(bf16)
    split[:, :CLASSES] = high
    split[:, LANES : LANES + CLASSES] = (values - high.astype(f32)).astype(bf16)


def split_coefs(coefs):
    return pl.pallas_call(
        split_kernel,
        out_shape=pltpu.VMEM((OWN, 2 * LANES), bf16),
        in_specs=[VMEM],
        out_specs=VMEM,
        compiler_params=pltpu.CompilerParams(vmem_limit_bytes=4 << 20),
        name="split_coefs",
    )(coefs)


def arrange_kernel(plan, n_in, *refs):
    for out, pieces in zip(refs[n_in:], plan):
        for source, row, out_row, out_col in pieces:
            out[out_row * OWN : (out_row + 1) * OWN, out_col * FEAT : (out_col + 1) * FEAT] = refs[source][
                row * OWN : (row + 1) * OWN, :
            ]


def arrange(outputs, name):
    arrays, plan, shapes = [], [], []

    def place(array):
        for i, known in enumerate(arrays):
            if known is array:
                return i
        arrays.append(array)
        return len(arrays) - 1

    for columns in outputs:
        plan.append(
            [
                (place(array), block, out_row, out_col)
                for out_col, column in enumerate(columns)
                for out_row, (array, block) in enumerate(column)
            ]
        )
        shapes.append(pltpu.VMEM((len(columns[0]) * OWN, len(columns) * FEAT), bf16))
    return pl.pallas_call(
        functools.partial(arrange_kernel, plan, len(arrays)),
        out_shape=shapes,
        in_specs=[VMEM] * len(arrays),
        out_specs=[VMEM] * len(shapes),
        compiler_params=pltpu.CompilerParams(vmem_limit_bytes=8 << 20),
        name=name,
    )(*arrays)


def block_rows(count):
    return 480 if count % 480 == 0 else count


def block_kernel(plan, n_in, parts, left_ready, apart, *refs):
    refs, (high, low) = refs[:-2], refs[-2:]
    inputs, refs = refs[:n_in], refs[n_in:]
    if left_ready:
        (left, split), refs = refs[:2], refs[2:]
    rights, totals = [None] * len(parts), [None] * len(parts)
    for i, (ready, _, _, total_row) in enumerate(parts):
        if ready:
            rights[i], refs = refs[0], refs[1:]
        if total_row is not None:
            totals[i], refs = refs[0], refs[1:]
    n_outs = sum(part[2] for part in parts) // OWN if apart else len(parts)
    outs, refs = refs[:n_outs], refs[n_outs:]
    if not left_ready:
        (left, split), refs = refs[:2], refs[2:]
    for i, (ready, _, _, _) in enumerate(parts):
        if not ready:
            rights[i], refs = refs[0], refs[1:]
    targets = (left, split, *rights)
    for target, out_row, out_col, source, row, col in plan:
        targets[target][out_row * OWN : (out_row + 1) * OWN, out_col * FEAT : (out_col + 1) * FEAT] = inputs[source][
            row * OWN : (row + 1) * OWN, col * FEAT : (col + 1) * FEAT
        ]
    done = 0
    for i, (_, first, count, total_row) in enumerate(parts):
        right = rights[i]
        rows = block_rows(count)
        for start in range(0, count, rows):
            n = slice(first + start, first + start + rows)
            for at in range(0, left.shape[0], 512):
                m = slice(at, min(at + 512, left.shape[0]))
                gram_a = dot(right[n, :FEAT], left[m, :FEAT], NT)
                gram_s = dot(right[n, FEAT:], left[m, FEAT:], NT)
                kernel = gram_a * gram_s
                rounded = kernel.astype(bf16)
                high[:rows, m] = rounded
                low[:rows, m] = (kernel - rounded.astype(f32)).astype(bf16)
            both = dot(high[:rows, :], split[...], NN)
            part = both[:, :LANES] + both[:, LANES:] + dot(low[:rows, :], split[:, :LANES], NN)
            if total_row is not None:
                part = part + totals[i][total_row + start : total_row + start + rows, :]
            if apart:
                for k in range(rows // OWN):
                    outs[done + k][...] = part[k * OWN : (k + 1) * OWN, :CLASSES]
                done += rows // OWN
            else:
                outs[i][start : start + rows, :] = part


def partial_sums(rights, left, apart, name):
    arrays, plan = [], []

    def place(array):
        for i, known in enumerate(arrays):
            if known is array:
                return i
        arrays.append(array)
        return len(arrays) - 1

    left_ready = isinstance(left, tuple)
    if not left_ready:
        for i, (act, sig, coef) in enumerate(left):
            plan.append((0, i, 0, place(act[0]), act[1], act[2]))
            plan.append((0, i, 1, place(sig[0]), sig[1], sig[2]))
            plan.append((1, i, 0, place(coef[0]), coef[1], coef[2]))
    for target, (blocks, *_) in enumerate(rights):
        if isinstance(blocks, list):
            for i, (act, sig) in enumerate(blocks):
                plan.append((2 + target, i, 0, place(act[0]), act[1], act[2]))
                plan.append((2 + target, i, 1, place(sig[0]), sig[1], sig[2]))
    n_in = len(arrays)
    left_rows = left[0].shape[0] if left_ready else len(left) * OWN
    if left_ready:
        arrays += left
    parts, laid = [], []
    for blocks, first, count, total, total_row in rights:
        ready = not isinstance(blocks, list)
        parts.append((ready, first, count, None if total is None else total_row))
        if ready:
            arrays.append(blocks)
        else:
            laid.append(pltpu.VMEM((len(blocks) * OWN, 2 * FEAT), bf16))
        if total is not None:
            arrays.append(total)
    if not left_ready:
        laid = [pltpu.VMEM((left_rows, 2 * FEAT), bf16), pltpu.VMEM((left_rows, 2 * LANES), bf16)] + laid
    if apart:
        sums = [pltpu.VMEM((OWN, CLASSES), f32)] * (sum(part[2] for part in parts) // OWN)
    else:
        sums = [pltpu.VMEM((part[2], LANES), f32) for part in parts]
    outs = pl.pallas_call(
        functools.partial(block_kernel, plan, n_in, parts, left_ready, apart),
        out_shape=sums + laid,
        in_specs=[VMEM] * len(arrays),
        out_specs=[VMEM] * (len(sums) + len(laid)),
        scratch_shapes=[pltpu.VMEM((max(block_rows(part[2]) for part in parts), left_rows), bf16)] * 2,
        cost_estimate=pl.CostEstimate(
            flops=sum(part[2] for part in parts) * left_rows * 5400, bytes_accessed=1_000_000, transcendentals=0
        ),
        compiler_params=pltpu.CompilerParams(vmem_limit_bytes=16 << 20),
        name=name,
    )(*arrays)
    return outs[: len(sums)], outs[len(sums) :]


def shards(activations, signals, labels, coefficients):
    coefs = coefficients.T
    groups = ("far", "near")
    a, s, c = {}, {}, {}
    for g in groups:
        a[g, "x"] = send(activations, g, "x")
        s[g, "y"] = send(signals, g, "y")
    c0 = split_coefs(coefs)
    cz = send(c0, "near", "z")
    act_own, sig_own = arrange([[[(after(v, c0), 0)]] for v in (activations, signals)], "own_rows")

    def together(*values):
        return lax.optimization_barrier(values)

    a["far", "x"], a["near", "x"], s["far", "y"], s["near", "y"], cz = together(
        a["far", "x"], a["near", "x"], s["far", "y"], s["near", "y"], cz
    )

    pairs = arrange(
        [[[(act_own, 0), (a[g, "x"], 0)]] for g in groups]
        + [[[(sig_own, 0), (s[g, "y"], 0)]] for g in groups]
        + [[[(c0, 0), (cz, 0)]]],
        "pairs",
    )
    a0x, s0y, c0z = dict(zip(groups, pairs[:2])), dict(zip(groups, pairs[2:4])), pairs[4]
    ay, sz = {}, {}
    for g in groups:
        ay[g] = send(a0x[g], g, "y")
        sz[g] = send(s0y[g], g, "z")
    cx = send(c0z, "near", "x")
    ay["far"], ay["near"], sz["far"], sz["near"], cx = together(ay["far"], ay["near"], sz["far"], sz["near"], cx)
    turned = arrange(
        [[[(a0x[g], k), (ay[g], k)]] for k in (0, 1) for g in groups],
        "turn",
    )
    a0y, axxy = dict(zip(groups, turned[:2])), dict(zip(groups, turned[2:]))
    az, sx = {}, {}
    for g in groups:
        sx[g] = send(after(s0y[g], sz[g]), g, "x")
    cy = send(after(c0z, cx), "near", "y")
    for g in groups:
        az[g] = send(a0y[g], g, "z")
    n = "near"
    (four,) = arrange(
        [
            [
                [(a0x[n], 0), (a0x[n], 1), (ay[n], 0), (ay[n], 1)],
                [(s0y[n], 0), (s0y[n], 1), (sz[n], 0), (sz[n], 1)],
                [(c0z, 0), (c0z, 1), (cx, 0), (cx, 1)],
            ]
        ],
        "four",
    )
    az["far"], az[n], sx["far"], sx[n], cy, four, axxy[n], sz[n], axxy["far"], sz["far"] = together(
        az["far"], az[n], sx["far"], sx[n], cy, four, axxy[n], sz[n], axxy["far"], sz["far"]
    )
    az_mate, sx_mate, cy_mate = small = [send(v, n, "c") for v in (az[n], sx[n], cy)]
    axz, sxz = {}, {}
    axz[n] = send(axxy[n], n, "z")
    sxz[n] = send(sz[n], n, "x")

    sxz["far"] = send(after(sz["far"], *small), "far", "x")
    four_mate = send(after(four, *small), n, "c")
    cxy = send(after(cx, *small), n, "y")
    axz["far"] = send(after(axxy["far"], four_mate), "far", "z")

    def blocks_of(g):
        act = {"": (a0x[g], 0, 0), "x": (a0x[g], 1, 0), "y": (ay[g], 0, 0), "xy": (ay[g], 1, 0)}
        act |= {"z": (az[g], 0, 0), "yz": (az[g], 1, 0), "xz": (axz[g], 0, 0), "xyz": (axz[g], 1, 0)}
        sig = {"": (s0y[g], 0, 0), "y": (s0y[g], 1, 0), "z": (sz[g], 0, 0), "yz": (sz[g], 1, 0)}
        sig |= {"x": (sx[g], 0, 0), "xy": (sx[g], 1, 0), "xz": (sxz[g], 0, 0), "xyz": (sxz[g], 1, 0)}
        return act, sig

    act, sig = blocks_of("far")
    right = {k: (act[k], sig[k]) for k in act}
    act, sig = blocks_of("near")
    coef = {"": (c0z, 0, 0), "z": (c0z, 1, 0), "x": (cx, 0, 0), "xz": (cx, 1, 0)}
    coef |= {"y": (cy, 0, 0), "yz": (cy, 1, 0), "xy": (cxy, 0, 0), "xyz": (cxy, 1, 0)}
    left = {k: (act[k], sig[k], coef[k]) for k in act}
    right_1 = [right[k] for k in ("xy", "yz", "x", "y", "z", "")]
    right_2 = [right[k] for k in ("xz", "xyz")]
    first, second = ("", "x", "y", "z", "yz"), ("xy", "xz", "xyz")

    coef[""] = (after(c0z, *small), 0, 0)
    act_mate = {"": (four_mate, 0, 0), "x": (four_mate, 1, 0), "y": (four_mate, 2, 0), "xy": (four_mate, 3, 0)}
    act_mate |= {"z": (az_mate, 0, 0), "yz": (az_mate, 1, 0)}
    sig_mate = {"": (four_mate, 0, 1), "y": (four_mate, 1, 1), "z": (four_mate, 2, 1), "yz": (four_mate, 3, 1)}
    sig_mate |= {"x": (sx_mate, 0, 0), "xy": (sx_mate, 1, 0)}
    coef_mate = {"": (four_mate, 0, 2), "z": (four_mate, 1, 2), "x": (four_mate, 2, 2), "xz": (four_mate, 3, 2)}
    coef_mate |= {"y": (cy_mate, 0, 0), "yz": (cy_mate, 1, 0)}
    left_1 = [(left[k][0], left[k][1], coef[k]) for k in first]
    left_1 += [(act_mate[k], sig_mate[k], coef_mate[k]) for k in first]
    (total_1,), (rows_1, coefs_1, wide_1) = partial_sums([(right_1, 0, 960, None, 0)], left_1, False, "early")
    axz_mate, sxz_mate = [send(after(v, total_1), n, "c") for v in (axz[n], sxz[n])]
    cxy_mate = send(after(cxy, total_1), n, "c")
    (total_2,), (wide_2,) = partial_sums(
        [(right_2, 0, 320, None, 0)], (after(rows_1, total_1), coefs_1), False, "early_right"
    )
    act_mate |= {"xz": (axz_mate, 0, 0), "xyz": (axz_mate, 1, 0)}
    sig_mate |= {"xz": (sxz_mate, 0, 0), "xyz": (sxz_mate, 1, 0)}
    coef_mate |= {"xy": (cxy_mate, 0, 0), "xyz": (cxy_mate, 1, 0)}
    left_2 = [left[k] for k in second]
    left_2 += [(act_mate[k], sig_mate[k], coef_mate[k]) for k in second]

    (sum_xyz,), (rows_2, coefs_2) = partial_sums([(wide_2, 160, 160, total_2, 160)], left_2, True, "second_farthest")
    got_xyz = send(sum_xyz, "far", "xyz")
    (sum_xz, sum_xy, sum_yz), _ = partial_sums(
        [(wide_2, 0, 160, total_2, 0), (wide_1, 0, 320, total_1, 0)], (rows_2, coefs_2), True, "second_far"
    )
    part_x, part_y, part_z = send(sum_xz, "far", "z"), send(sum_xy, "far", "x"), send(sum_yz, "far", "y")
    (sum_x, sum_y, sum_z), _ = partial_sums(
        [(wide_1, 320, 480, total_1, 320)], (after(rows_2, sum_xz, got_xyz), coefs_2), True, "second_near"
    )
    got_x = send(after(sum_x + part_x, sum_z), "far", "x")
    got_y = send(after(sum_y + part_y, sum_z), "far", "y")
    last = sum_z + part_z
    got_z = send(last, "far", "z")
    (own,), _ = partial_sums([(wide_1, 800, 160, total_1, 800)], (after(rows_2, last), coefs_2), True, "second_here")

    product = own + got_xyz + got_x + got_y + got_z
    product = product * (1.0 / (FEAT * FEAT))
    classes = jnp.arange(CLASSES, dtype=jnp.int32)
    targets = (labels[:, None] == classes[None, :]).astype(f32) - 1.0 / CLASSES
    return (coefs + damping * (targets - product - ridge * coefs)).T


def solution(mesh):
    in_specs = (P(AXES, None), P(AXES, None), P(AXES), P(None, AXES))
    return jax.shard_map(shards, mesh=mesh, in_specs=in_specs, out_specs=P(None, AXES), check_vma=False)
```
